32 devices in a mesh: cls: 2 (over y), pts: 4 (over z), sub: 2 (over x), rep: 2 (over core).
Axes of the slice: x: 2, y: 2, z: 4, core: 2. Of those that a mesh axis runs over, the one named last changes fastest.
Arguments:
- right_sides: bfloat16 [128, 131072], P('rep', ('cls', 'pts', 'sub')), parts along dimension 1, may hold values from -6 to 6
- curve_order: int32 [16, 8192], P(('cls', 'pts', 'sub')), parts along dimension 0, may hold values from 0 to 8191, each once within a row
- level_bases: bfloat16 [4, 128, 131072], P(None, 'rep', ('cls', 'pts', 'sub')), parts along dimension 2, may hold values from -0.0234375 to 0.0234375
- capacitance: float32 [30, 256, 256], P('cls'), parts along dimension 0
Outputs:
- solved: bfloat16 [128, 131072], P('rep', ('cls', 'pts', 'sub')), parts along dimension 1
The draws below stay inside these ranges and needn't reach their ends.
There are 2 independent parts, one for each index of `cls`. The reference program is written for one: setup_inputs(seed, part) draws one part's arguments, and reference() takes and returns one part's arrays. A program takes and returns all parts, laid end to end along the dimension named above; each array names one. Nothing has to cross between parts.
All inputs are finite; a program needn't handle non-finite values.
Results may differ from the reference program's by a relative error of at most 0.014.
Values may be sent and summed in bfloat16 or wider, within the bound.
A program may use at most 64 MiB of HBM per device.

```python
import math
import jax
import jax.numpy as jnp
from jax import lax

RANK = 128
RHS = 128
LEVELS = 4
NPD = 8192
BLOCKS = 8
N_ALL = 65536
PARENTS = 15


def draw_capacitance(key, part):
    doubled = 2 * RANK
    first_key, second_key = jax.random.split(key)
    identity = jnp.eye(doubled, dtype=jnp.float32)
    diagonal = jax.random.uniform(first_key, (PARENTS, doubled, 1), jnp.float32, 0.5, 1.5)
    spread = jnp.clip(jax.random.normal(second_key, (PARENTS, doubled, doubled), jnp.float32), -3.0, 3.0) * (0.25 / math.sqrt(doubled))
    return identity * diagonal + (1.0 - identity) * spread


def shard_levels(own_key, shape, pieces, least, high):
    factor_of, own = 1.0, jax.random.fold_in(own_key, 6)
    for dim, blocks in pieces:
        steps = jnp.exp(jax.random.uniform(jax.random.fold_in(own, dim), (blocks,), jnp.float32, least / len(pieces), high / len(pieces)))
        factor_of = factor_of * jnp.repeat(steps, shape[dim] // blocks).reshape([-1 if axis == dim else 1 for axis in range(len(shape))])
    return factor_of


def noise(own_key, extent, scale, reach, pieces=(), kind=jnp.bfloat16):
    entries = jax.random.normal(own_key, extent, jnp.float32) * scale
    if len(pieces) > 0:
        entries = shard_levels(own_key, extent, pieces, -0.22, 0.18) * entries
    return jnp.clip(entries, min=-reach, max=reach).astype(kind)


def setup_inputs(seed: int = 0, part: int = 0) -> dict:
    splits = jax.random.split(jax.random.key(seed), 5)
    part_keys = jax.random.split(jax.random.fold_in(splits[4], part), 5)
    right_sides = noise(part_keys[0], (RHS, N_ALL), 1.0, 6.0, ((0, 2), (1, 8)))
    curve_order = jax.vmap(lambda own: jax.random.permutation(own, NPD))(jax.random.split(part_keys[1], BLOCKS)).reshape((BLOCKS, NPD)).astype(jnp.int32)
    level_bases = noise(part_keys[2], (LEVELS, RANK, N_ALL), N_ALL ** -0.5, 0.0234375, ((1, 2), (2, 8)))
    capacitance = draw_capacitance(jax.random.fold_in(jax.random.fold_in(splits[4], part), 71), part)
    return dict(right_sides=right_sides, curve_order=curve_order, level_bases=level_bases, capacitance=capacitance)


def reference(right_sides, curve_order, level_bases, capacitance):
    rhs_rows = right_sides.shape[0]
    total_points = right_sides.shape[1]
    shaped = right_sides.reshape(rhs_rows, BLOCKS, NPD)
    picked = jnp.take_along_axis(shaped, jnp.broadcast_to(curve_order[None], shaped.shape), axis=2)
    current = picked.reshape(rhs_rows, total_points).astype(jnp.float32)
    for tree_level in range(LEVELS, 0, -1):
        node_count = 2 ** tree_level
        node_size = total_points // node_count
        level_basis = level_bases[tree_level - 1].reshape(RANK, node_count, node_size).transpose(1, 0, 2)
        rounded = current.astype(jnp.bfloat16).reshape(rhs_rows, node_count, node_size).transpose(1, 0, 2)

        def project(pair_args):
            node_rows, node_basis = pair_args
            return lax.dot_general(node_rows, node_basis, (((1,), (1,)), ((), ())), preferred_element_type=jnp.float32)
        projections = lax.map(project, (rounded, level_basis))
        parent_count = node_count // 2
        stacked = projections.reshape(parent_count, 2, rhs_rows, RANK).transpose(0, 2, 1, 3).reshape(parent_count, rhs_rows, 2 * RANK)
        cap_blocks = capacitance[parent_count - 1:node_count - 1]
        factor = 0.3 * node_count * math.sqrt(node_size / RANK)
        coefficients = jnp.einsum('prb,pab->pra', stacked, cap_blocks, precision=lax.Precision.HIGHEST) * factor
        coefficients = coefficients.astype(jnp.bfloat16)
        coefficients = coefficients.reshape(parent_count, rhs_rows, 2, RANK).transpose(0, 2, 1, 3).reshape(node_count, rhs_rows, RANK)

        def correct(pair_args):
            node_coeff, node_basis = pair_args
            return jnp.dot(node_coeff, node_basis, preferred_element_type=jnp.float32)
        update = lax.map(correct, (coefficients, level_basis))
        current = current - update.transpose(1, 0, 2).reshape(rhs_rows, total_points)
    return current.astype(jnp.bfloat16)
```

```python
import functools
import math

import jax
import jax.numpy as jnp
from jax import lax
from jax.experimental import pallas as pl
from jax.experimental.pallas import tpu as pltpu
from jax.sharding import PartitionSpec as P

RANK = 128
LEVELS = 4
LANES = 128
CHUNK = 2048
STAGE_BITS = 2
MESH = pl.DeviceIdType.MESH
F32 = jnp.float32
BF16 = jnp.bfloat16


def dot_nt(a, b):
    return lax.dot_general(a, b, (((1,), (1,)), ((), ())), preferred_element_type=F32)


def gather_kernel(order, x, out, table, rows_a, rows_b):
    rhs, points = x.shape
    blocks = points // LANES

    @pl.loop(0, blocks, unroll=4)
    def _(b):
        cols = pl.ds(pl.multiple_of(b * LANES, LANES), LANES)
        table[cols, 0:rhs] = x[:, cols].astype(F32).T

    def pick(b, rows):
        for j in range(LANES):
            rows[pl.ds(j, 1), :] = table[pl.ds(order[0, b * LANES + j], 1), :]

    def put(b, rows):
        cols = pl.ds(pl.multiple_of(b * LANES, LANES), LANES)
        out[:, cols] = rows[...].T[0:rhs].astype(BF16)

    pick(0, rows_a)

    @pl.loop(0, blocks // 2 - 1)
    def _(i):
        pick(2 * i + 1, rows_b)
        put(2 * i, rows_a)
        pick(2 * i + 2, rows_a)
        put(2 * i + 1, rows_b)

    pick(blocks - 1, rows_b)
    put(blocks - 2, rows_a)
    put(blocks - 1, rows_b)


def gather(order, x):
    rhs, points = x.shape
    return pl.pallas_call(
        gather_kernel,
        out_shape=jax.ShapeDtypeStruct((rhs, points), BF16),
        in_specs=[
            pl.BlockSpec(memory_space=pltpu.SMEM),
            pl.BlockSpec(memory_space=pltpu.VMEM),
        ],
        out_specs=pl.BlockSpec(memory_space=pltpu.VMEM),
        scratch_shapes=[
            pltpu.VMEM((points, LANES), F32),
            pltpu.VMEM((LANES, LANES), F32),
            pltpu.VMEM((LANES, LANES), F32),
        ],
        compiler_params=pltpu.CompilerParams(vmem_limit_bytes=24 * 2**20),
        cost_estimate=pl.CostEstimate(
            flops=points * LANES * 64, bytes_accessed=16 * rhs * points, transcendentals=0
        ),
        name="curve_gather",
    )(order, x)


def plan(points, total):
    levels, slot = [], 0
    for level in range(LEVELS, 0, -1):
        size = total // 2**level
        span, local = max(size // points, 1), max(points // size, 1)
        stages = []
        if local == 1:
            sibling = span.bit_length() - 1
            bits = list(range(sibling + 1))
            for at in range(0, len(bits), STAGE_BITS):
                group = bits[at : at + STAGE_BITS]
                masks = []
                for mix in range(1, 2 ** len(group)):
                    mask = sum(1 << bit for i, bit in enumerate(group) if mix >> i & 1)
                    masks.append((mask, bool(mask >> sibling & 1), slot))
                    slot += 1
                stages.append(masks)
        factor = 0.3 * 2**level * math.sqrt(size / RANK)
        levels.append((level, span, local, stages, factor))
    return levels, slot


def split(value):
    high = value.astype(BF16)
    return high, (value - high.astype(F32)).astype(BF16)


def solve_kernel(
    levels, x, own, other, cap, out, current, basis, caps, send, recv,
    basis_sems, cap_sems, send_sems, recv_sems,
):
    rhs, points = x.shape
    half = own.shape[1]
    sub_size = lax.axis_size("sub")
    sub_bits = sub_size.bit_length() - 1
    pts, sub = lax.axis_index("pts"), lax.axis_index("sub")
    rep = lax.axis_index("rep")
    block = pts * sub_size + sub

    def partner(mask):
        def flip(value, bits):
            for i in range(bits.bit_length()):
                if bits >> i & 1:
                    value = value + (1 << i) * (1 - 2 * (value // (1 << i) % 2))
            return value

        return {"pts": flip(pts, mask >> sub_bits), "sub": flip(sub, mask & sub_size - 1)}

    masks = sorted({m for _, _, _, stages, _ in levels for stage in stages for m, _, _ in stage})
    barrier = pltpu.get_barrier_semaphore()
    for mask in masks:
        pl.semaphore_signal(barrier, inc=1, device_id=partner(mask), device_id_type=MESH)

    basis_copies, cap_copies = [], []
    for n, (level, span, local, _, _) in enumerate(levels):
        first = block // span * local
        parent = 2 ** (level - 1) - 1 + first // 2
        odd = first % 2
        copies = []
        for piece, source in enumerate((own, other)):
            row = rep * half if piece == 0 else (1 - rep) * half
            copies.append(
                pltpu.make_async_copy(
                    source.at[level - 1],
                    basis.at[n, pl.ds(pl.multiple_of(row, half), half), :],
                    basis_sems.at[n, piece],
                )
            )
        basis_copies.append(copies)
        if local == 1:
            mine = pl.ds(pl.multiple_of(odd * RANK, RANK), RANK)
            theirs = pl.ds(pl.multiple_of((1 - odd) * RANK, RANK), RANK)
            cap_copies.append(
                [
                    pltpu.make_async_copy(
                        cap.at[parent, mine, cols],
                        caps.at[n, 0:RANK, piece * RANK : (piece + 1) * RANK],
                        cap_sems.at[n, piece],
                    )
                    for piece, cols in enumerate((mine, theirs))
                ]
            )
        else:
            cap_copies.append([pltpu.make_async_copy(cap.at[parent], caps.at[n], cap_sems.at[n, 0])])
        for copy in copies + cap_copies[-1]:
            copy.start()

    def chunk(i):
        return pl.ds(pl.multiple_of(i * CHUNK, CHUNK), CHUNK)

    steps = points // CHUNK

    def wait_basis(n):
        for copy in basis_copies[n]:
            copy.wait()

    wait_basis(0)
    local = levels[0][2]
    per_node = steps // local
    sums = []
    for node in range(local):
        def first_step(i, total):
            return total + dot_nt(x[:, chunk(i)], basis[0, :, chunk(i)])

        sums.append(
            lax.fori_loop(
                node * per_node, (node + 1) * per_node, first_step, jnp.zeros((rhs, RANK), F32)
            )
        )

    barrier_waited = False
    for n, (level, span, local, stages, factor) in enumerate(levels):
        for copy in cap_copies[n]:
            copy.wait()
        if local > 1:
            s = jnp.concatenate(sums, axis=1)
            c = caps[n]
        else:
            total = sums[0]
            sibling = None
            c = caps[n, 0:RANK, :]
            for stage in stages:
                if not barrier_waited:
                    pl.semaphore_wait(barrier, len(masks))
                    barrier_waited = True
                slot0 = stage[0][2]
                send[slot0] = total.astype(BF16)
                copies = []
                for mask, crosses, slot in stage:
                    copy = pltpu.make_async_remote_copy(
                        src_ref=send.at[slot0],
                        dst_ref=recv.at[slot],
                        send_sem=send_sems.at[slot],
                        recv_sem=recv_sems.at[slot],
                        device_id=partner(mask),
                        device_id_type=MESH,
                    )
                    copy.start()
                    copies.append(copy)
                for copy, (mask, crosses, slot) in zip(copies, stage):
                    copy.wait()
                    value = recv[slot].astype(F32)
                    if crosses:
                        sibling = value if sibling is None else sibling + value
                    else:
                        total = total + value
            s = jnp.concatenate([total, sibling], axis=1)
        c_high, c_low = split(c)
        s_high, s_low = split(s)
        coefficients = dot_nt(s_high, c_high) + dot_nt(s_low, c_high) + dot_nt(s_high, c_low)
        coefficients = (coefficients * factor).astype(BF16)
        before = x if n == 0 else current
        last = n == LEVELS - 1
        if not last:
            wait_basis(n + 1)
            next_local = levels[n + 1][2]
        pieces = max(local, 1 if last else next_local)
        width = steps // pieces
        sums = []
        for piece in range(pieces):
            node = piece * local // pieces
            mine = coefficients[:, node * RANK : (node + 1) * RANK]

            def step(i, total):
                here = chunk(i)
                update = jnp.dot(mine, basis[n, :, here], preferred_element_type=F32)
                value = before[:, here].astype(F32) - update
                if last:
                    out[:, here] = value.astype(BF16)
                    return total
                current[:, here] = value
                return total + dot_nt(value.astype(BF16), basis[n + 1, :, here])

            total = lax.fori_loop(
                piece * width, (piece + 1) * width, step, jnp.zeros((rhs, RANK), F32)
            )
            sums.append(total)
        if not last:
            group = pieces // next_local
            sums = [sum(sums[i * group + 1 : (i + 1) * group], sums[i * group]) for i in range(next_local)]


def shards(right_sides, curve_order, level_bases, capacitance):
    rhs, points = right_sides.shape
    total = points * lax.axis_size(("pts", "sub"))
    levels, slots = plan(points, total)
    other = lax.ppermute(level_bases, "rep", [(0, 1), (1, 0)])
    permuted = gather(curve_order, right_sides)
    hbm = pl.BlockSpec(memory_space=pl.ANY)
    vmem = pl.BlockSpec(memory_space=pltpu.VMEM)
    return pl.pallas_call(
        functools.partial(solve_kernel, levels),
        out_shape=jax.ShapeDtypeStruct((rhs, points), BF16),
        in_specs=[vmem, hbm, hbm, hbm],
        out_specs=vmem,
        scratch_shapes=[
            pltpu.VMEM((rhs, points), F32),
            pltpu.VMEM((LEVELS, RANK, points), BF16),
            pltpu.VMEM((LEVELS, 2 * RANK, 2 * RANK), F32),
            pltpu.VMEM((slots, rhs, RANK), BF16),
            pltpu.VMEM((slots, rhs, RANK), BF16),
            pltpu.SemaphoreType.DMA((LEVELS, 2)),
            pltpu.SemaphoreType.DMA((LEVELS, 2)),
            pltpu.SemaphoreType.DMA((slots,)),
            pltpu.SemaphoreType.DMA((slots,)),
        ],
        compiler_params=pltpu.CompilerParams(
            collective_id=0, has_side_effects=True, vmem_limit_bytes=32 * 2**20
        ),
        cost_estimate=pl.CostEstimate(
            flops=16 * rhs * RANK * points, bytes_accessed=20 * 2**20, transcendentals=0
        ),
        name="tree_solve",
    )(permuted, level_bases, other, capacitance)


def solution(mesh):
    in_specs = (
        P("rep", ("cls", "pts", "sub")),
        P(("cls", "pts", "sub"), None),
        P(None, "rep", ("cls", "pts", "sub")),
        P("cls", None, None),
    )
    out_specs = P("rep", ("cls", "pts", "sub"))
    return jax.shard_map(shards, mesh=mesh, in_specs=in_specs, out_specs=out_specs, check_vma=False)
```

```python
import functools
import math

import jax
import jax.numpy as jnp
from jax import lax
from jax.experimental import pallas as pl
from jax.experimental.pallas import tpu as pltpu
from jax.sharding import PartitionSpec as P

RANK = 128
LEVELS = 4
LANES = 128
CHUNK = 1024
PIECES = 4
STAGE_BITS = 2
MESH = pl.DeviceIdType.MESH
F32 = jnp.float32
BF16 = jnp.bfloat16


def dot_nt(a, b):
    return lax.dot_general(a, b, (((1,), (1,)), ((), ())), preferred_element_type=F32)


def plan(points, total):
    levels, slot = [], 0
    for level in range(LEVELS, 0, -1):
        size = total // 2**level
        span, local = max(size // points, 1), max(points // size, 1)
        stages = []
        if local == 1:
            sibling = span.bit_length() - 1
            bits = list(range(sibling + 1))
            for at in range(0, len(bits), STAGE_BITS):
                group = bits[at : at + STAGE_BITS]
                masks = []
                for mix in range(1, 2 ** len(group)):
                    mask = sum(1 << bit for i, bit in enumerate(group) if mix >> i & 1)
                    masks.append((mask, bool(mask >> sibling & 1), slot))
                    slot += 1
                stages.append(masks)
        factor = 0.3 * 2**level * math.sqrt(size / RANK)
        levels.append((level, span, local, stages, factor))
    return levels, slot


def split(value):
    high = value.astype(BF16)
    return high, (value - high.astype(F32)).astype(BF16)


def gather(order, x, out, table, rows_a, rows_b):
    rhs, points = x.shape
    blocks = points // LANES

    def pick(b, rows):
        for j in range(LANES):
            rows[pl.ds(j, 1), :] = table[pl.ds(order[0, b * LANES + j], 1), :]

    def put(b, rows):
        cols = pl.ds(pl.multiple_of(b * LANES, LANES), LANES)
        out[:, cols] = rows[...].T[0:rhs].astype(BF16)

    pick(0, rows_a)

    @pl.loop(0, blocks // 2 - 1)
    def _(i):
        pick(2 * i + 1, rows_b)
        put(2 * i, rows_a)
        pick(2 * i + 2, rows_a)
        put(2 * i + 1, rows_b)

    pick(blocks - 1, rows_b)
    put(blocks - 2, rows_a)
    put(blocks - 1, rows_b)


def solve_kernel(
    levels, sides, order_in, own, cap, out,
    raw, order, x, table, rows_a, rows_b, current, basis, caps, result, send, recv,
    in_sems, basis_sems, far_send_sems, far_recv_sems, cap_sems, out_sems, send_sems, recv_sems,
):
    rhs, points = raw.shape
    half = own.shape[1]
    sub_size = lax.axis_size("sub")
    sub_bits = sub_size.bit_length() - 1
    pts, sub = lax.axis_index("pts"), lax.axis_index("sub")
    rep = lax.axis_index("rep")
    block = pts * sub_size + sub

    def partner(mask):
        def flip(value, bits):
            for i in range(bits.bit_length()):
                if bits >> i & 1:
                    value = value + (1 << i) * (1 - 2 * (value // (1 << i) % 2))
            return value

        return {"pts": flip(pts, mask >> sub_bits), "sub": flip(sub, mask & sub_size - 1)}

    masks = sorted({m for _, _, _, stages, _ in levels for stage in stages for m, _, _ in stage})
    barrier = pltpu.get_barrier_semaphore()
    pl.semaphore_signal(barrier, inc=1, device_id={"rep": 1 - rep}, device_id_type=MESH)
    for mask in masks:
        pl.semaphore_signal(barrier, inc=1, device_id=partner(mask), device_id_type=MESH)

    piece_width = points // PIECES
    side_copies = []
    for piece in range(PIECES):
        cols = pl.ds(piece * piece_width, piece_width)
        side_copies.append(
            pltpu.make_async_copy(sides.at[:, cols], raw.at[:, cols], in_sems.at[piece])
        )
        side_copies[-1].start()
    order_copy = pltpu.make_async_copy(order_in, order, in_sems.at[PIECES])
    order_copy.start()

    basis_copies, cap_copies = [], []
    for n, (level, span, local, _, _) in enumerate(levels):
        first = block // span * local
        parent = 2 ** (level - 1) - 1 + first // 2
        odd = first % 2
        mine_at = basis.at[n, pl.ds(pl.multiple_of(rep * half, half), half), :]
        here = pltpu.make_async_copy(own.at[level - 1], mine_at, basis_sems.at[n])
        far = pltpu.make_async_remote_copy(
            src_ref=own.at[level - 1],
            dst_ref=mine_at,
            send_sem=far_send_sems.at[n],
            recv_sem=far_recv_sems.at[n],
            device_id={"rep": 1 - rep},
            device_id_type=MESH,
        )
        basis_copies.append((here, far))
        if local == 1:
            mine = pl.ds(pl.multiple_of(odd * RANK, RANK), RANK)
            theirs = pl.ds(pl.multiple_of((1 - odd) * RANK, RANK), RANK)
            cap_copies.append(
                [
                    pltpu.make_async_copy(
                        cap.at[parent, mine, cols],
                        caps.at[n, 0:RANK, piece * RANK : (piece + 1) * RANK],
                        cap_sems.at[n, piece],
                    )
                    for piece, cols in enumerate((mine, theirs))
                ]
            )
        else:
            cap_copies.append([pltpu.make_async_copy(cap.at[parent], caps.at[n], cap_sems.at[n, 0])])
        for copy in [here] + cap_copies[-1]:
            copy.start()

    for piece in range(PIECES):
        side_copies[piece].wait()

        @pl.loop(piece * piece_width // LANES, (piece + 1) * piece_width // LANES, unroll=4)
        def _(b):
            cols = pl.ds(pl.multiple_of(b * LANES, LANES), LANES)
            table[cols, 0:rhs] = raw[:, cols].astype(F32).T

    pl.semaphore_wait(barrier, len(masks) + 1)
    for _, far in basis_copies:
        far.start()
    order_copy.wait()
    gather(order, raw, x, table, rows_a, rows_b)

    def chunk(i):
        return pl.ds(pl.multiple_of(i * CHUNK, CHUNK), CHUNK)

    steps = points // CHUNK

    def wait_basis(n):
        for copy in basis_copies[n]:
            copy.wait()

    wait_basis(0)
    local = levels[0][2]
    per_node = steps // local
    sums = []
    for node in range(local):
        def first_step(i, total):
            return total + dot_nt(x[:, chunk(i)], basis[0, :, chunk(i)])

        sums.append(
            lax.fori_loop(
                node * per_node, (node + 1) * per_node, first_step, jnp.zeros((rhs, RANK), F32)
            )
        )

    for n, (level, span, local, stages, factor) in enumerate(levels):
        for copy in cap_copies[n]:
            copy.wait()
        if local > 1:
            s = jnp.concatenate(sums, axis=1)
            c = caps[n]
        else:
            total = sums[0]
            sibling = None
            c = caps[n, 0:RANK, :]
            for stage in stages:
                slot0 = stage[0][2]
                send[slot0] = total.astype(BF16)
                copies = []
                for mask, crosses, slot in stage:
                    copy = pltpu.make_async_remote_copy(
                        src_ref=send.at[slot0],
                        dst_ref=recv.at[slot],
                        send_sem=send_sems.at[slot],
                        recv_sem=recv_sems.at[slot],
                        device_id=partner(mask),
                        device_id_type=MESH,
                    )
                    copy.start()
                    copies.append(copy)
                for copy, (mask, crosses, slot) in zip(copies, stage):
                    copy.wait()
                    value = recv[slot].astype(F32)
                    if crosses:
                        sibling = value if sibling is None else sibling + value
                    else:
                        total = total + value
            s = jnp.concatenate([total, sibling], axis=1)
        c_high, c_low = split(c)
        s_high, s_low = split(s)
        coefficients = dot_nt(s_high, c_high) + dot_nt(s_low, c_high) + dot_nt(s_high, c_low)
        coefficients = (coefficients * factor).astype(BF16)
        before = x if n == 0 else current
        last = n == LEVELS - 1
        if not last:
            wait_basis(n + 1)
            next_local = levels[n + 1][2]
        pieces = max(local, 1 if last else next_local)
        width = steps // pieces
        sums = []
        for piece in range(pieces):
            node = piece * local // pieces
            mine = coefficients[:, node * RANK : (node + 1) * RANK]

            def step(i, total):
                here = chunk(i)
                update = jnp.dot(mine, basis[n, :, here], preferred_element_type=F32)
                value = before[:, here].astype(F32) - update
                if last:
                    result[:, here] = value.astype(BF16)
                    return total
                current[:, here] = value
                return total + dot_nt(value.astype(BF16), basis[n + 1, :, here])

            if last:
                out_copies = []
                for part in range(PIECES):
                    for i in range(part * steps // PIECES, (part + 1) * steps // PIECES):
                        step(i, None)
                    cols = pl.ds(part * piece_width, piece_width)
                    out_copies.append(
                        pltpu.make_async_copy(result.at[:, cols], out.at[:, cols], out_sems.at[part])
                    )
                    out_copies[-1].start()
                for copy in out_copies:
                    copy.wait()
                return
            total = lax.fori_loop(
                piece * width, (piece + 1) * width, step, jnp.zeros((rhs, RANK), F32)
            )
            sums.append(total)
        group = pieces // next_local
        sums = [sum(sums[i * group + 1 : (i + 1) * group], sums[i * group]) for i in range(next_local)]


def shards(right_sides, curve_order, level_bases, capacitance):
    rhs, points = right_sides.shape
    total = points * lax.axis_size(("pts", "sub"))
    levels, slots = plan(points, total)
    hbm = pl.BlockSpec(memory_space=pltpu.MemorySpace.HBM)
    return pl.pallas_call(
        functools.partial(solve_kernel, levels),
        out_shape=jax.ShapeDtypeStruct((rhs, points), BF16),
        in_specs=[hbm, hbm, hbm, hbm],
        out_specs=hbm,
        scratch_shapes=[
            pltpu.VMEM((rhs, points), BF16),
            pltpu.SMEM((1, points), jnp.int32),
            pltpu.VMEM((rhs, points), BF16),
            pltpu.VMEM((points, LANES), F32),
            pltpu.VMEM((LANES, LANES), F32),
            pltpu.VMEM((LANES, LANES), F32),
            pltpu.VMEM((rhs, points), F32),
            pltpu.VMEM((LEVELS, RANK, points), BF16),
            pltpu.VMEM((LEVELS, 2 * RANK, 2 * RANK), F32),
            pltpu.VMEM((rhs, points), BF16),
            pltpu.VMEM((slots, rhs, RANK), BF16),
            pltpu.VMEM((slots, rhs, RANK), BF16),
            pltpu.SemaphoreType.DMA((PIECES + 1,)),
            pltpu.SemaphoreType.DMA((LEVELS,)),
            pltpu.SemaphoreType.DMA((LEVELS,)),
            pltpu.SemaphoreType.DMA((LEVELS,)),
            pltpu.SemaphoreType.DMA((LEVELS, 2)),
            pltpu.SemaphoreType.DMA((PIECES,)),
            pltpu.SemaphoreType.DMA((slots,)),
            pltpu.SemaphoreType.DMA((slots,)),
        ],
        compiler_params=pltpu.CompilerParams(
            collective_id=0, has_side_effects=True, vmem_limit_bytes=48 * 2**20
        ),
        cost_estimate=pl.CostEstimate(
            flops=16 * rhs * RANK * points, bytes_accessed=20 * 2**20, transcendentals=0
        ),
        name="tree_solve",
    )(right_sides, curve_order, level_bases, capacitance)


def solution(mesh):
    in_specs = (
        P("rep", ("cls", "pts", "sub")),
        P(("cls", "pts", "sub"), None),
        P(None, "rep", ("cls", "pts", "sub")),
        P("cls", None, None),
    )
    out_specs = P("rep", ("cls", "pts", "sub"))
    return jax.shard_map(shards, mesh=mesh, in_specs=in_specs, out_specs=out_specs, check_vma=False)
```

```python
import functools
import math

import jax
import jax.numpy as jnp
from jax import lax
from jax.experimental import pallas as pl
from jax.experimental.pallas import tpu as pltpu
from jax.sharding import PartitionSpec as P

RANK = 128
LEVELS = 4
LANES = 128
CHUNK = 1024
PIECES = 4
STAGE_BITS = 2
MESH = pl.DeviceIdType.MESH
F32 = jnp.float32
BF16 = jnp.bfloat16


def dot_nt(a, b):
    return lax.dot_general(a, b, (((1,), (1,)), ((), ())), preferred_element_type=F32)


def plan(points, total):
    levels, slot = [], 0
    for level in range(LEVELS, 0, -1):
        size = total // 2**level
        span, local = max(size // points, 1), max(points // size, 1)
        stages = []
        if local == 1:
            sibling = span.bit_length() - 1
            bits = list(range(sibling + 1))
            for at in range(0, len(bits), STAGE_BITS):
                group = bits[at : at + STAGE_BITS]
                masks = []
                for mix in range(1, 2 ** len(group)):
                    mask = sum(1 << bit for i, bit in enumerate(group) if mix >> i & 1)
                    masks.append((mask, bool(mask >> sibling & 1), slot))
                    slot += 1
                stages.append(masks)
        factor = 0.3 * 2**level * math.sqrt(size / RANK)
        levels.append((level, span, local, stages, factor))
    return levels, slot


def split(value):
    high = value.astype(BF16)
    return high, (value - high.astype(F32)).astype(BF16)


def gather(order, x, out, table, rows_a, rows_b, first, stop):
    rhs = x.shape[0]

    def pick(b, rows):
        for j in range(LANES):
            rows[pl.ds(j, 1), :] = table[pl.ds(order[0, b * LANES + j], 1), :]

    def put(b, rows):
        cols = pl.ds(pl.multiple_of(b * LANES, LANES), LANES)
        out[:, cols] = rows[...].T[0:rhs].astype(BF16)

    pick(first, rows_a)

    @pl.loop(first // 2, stop // 2 - 1)
    def _(i):
        pick(2 * i + 1, rows_b)
        put(2 * i, rows_a)
        pick(2 * i + 2, rows_a)
        put(2 * i + 1, rows_b)

    pick(stop - 1, rows_b)
    put(stop - 2, rows_a)
    put(stop - 1, rows_b)


def solve_kernel(
    levels, sides, order_in, own, cap, out,
    raw, order, x, table, rows_a, rows_b, current, basis, caps, result, send, recv,
    in_sems, basis_sems, far_send_sems, far_recv_sems, cap_sems, out_sems, send_sems, recv_sems,
):
    rhs, points = raw.shape
    half = own.shape[1]
    sub_size = lax.axis_size("sub")
    sub_bits = sub_size.bit_length() - 1
    pts, sub = lax.axis_index("pts"), lax.axis_index("sub")
    rep = lax.axis_index("rep")
    block = pts * sub_size + sub

    def partner(mask):
        def flip(value, bits):
            for i in range(bits.bit_length()):
                if bits >> i & 1:
                    value = value + (1 << i) * (1 - 2 * (value // (1 << i) % 2))
            return value

        return {"pts": flip(pts, mask >> sub_bits), "sub": flip(sub, mask & sub_size - 1)}

    masks = sorted({m for _, _, _, stages, _ in levels for stage in stages for m, _, _ in stage})
    barrier = pltpu.get_barrier_semaphore()
    pl.semaphore_signal(barrier, inc=1, device_id={"rep": 1 - rep}, device_id_type=MESH)
    for mask in masks:
        pl.semaphore_signal(barrier, inc=1, device_id=partner(mask), device_id_type=MESH)

    piece_width = points // PIECES
    side_copies = []
    for piece in range(PIECES):
        cols = pl.ds(piece * piece_width, piece_width)
        side_copies.append(
            pltpu.make_async_copy(sides.at[:, cols], raw.at[:, cols], in_sems.at[piece])
        )
        side_copies[-1].start()
    order_copy = pltpu.make_async_copy(order_in, order, in_sems.at[PIECES])
    order_copy.start()

    basis_copies, cap_copies = [], []
    for n, (level, span, local, _, _) in enumerate(levels):
        first = block // span * local
        parent = 2 ** (level - 1) - 1 + first // 2
        odd = first % 2
        mine_at = basis.at[n, pl.ds(pl.multiple_of(rep * half, half), half), :]
        here = pltpu.make_async_copy(own.at[level - 1], mine_at, basis_sems.at[n])
        far = pltpu.make_async_remote_copy(
            src_ref=own.at[level - 1],
            dst_ref=mine_at,
            send_sem=far_send_sems.at[n],
            recv_sem=far_recv_sems.at[n],
            device_id={"rep": 1 - rep},
            device_id_type=MESH,
        )
        basis_copies.append((here, far))
        if local == 1:
            mine = pl.ds(pl.multiple_of(odd * RANK, RANK), RANK)
            theirs = pl.ds(pl.multiple_of((1 - odd) * RANK, RANK), RANK)
            cap_copies.append(
                [
                    pltpu.make_async_copy(
                        cap.at[parent, mine, cols],
                        caps.at[n, 0:RANK, piece * RANK : (piece + 1) * RANK],
                        cap_sems.at[n, piece],
                    )
                    for piece, cols in enumerate((mine, theirs))
                ]
            )
        else:
            cap_copies.append([pltpu.make_async_copy(cap.at[parent], caps.at[n], cap_sems.at[n, 0])])
        for copy in [here] + cap_copies[-1]:
            copy.start()

    def share_basis():
        pl.semaphore_wait(barrier, len(masks) + 1)
        for _, far in basis_copies:
            far.start()

    @pl.when(rep != 0)
    def _():
        share_basis()

    for piece in range(PIECES):
        side_copies[piece].wait()

        @pl.loop(piece * piece_width // LANES, (piece + 1) * piece_width // LANES, unroll=4)
        def _(b):
            cols = pl.ds(pl.multiple_of(b * LANES, LANES), LANES)
            table[cols, 0:rhs] = raw[:, cols].astype(F32).T

    order_copy.wait()
    gather(order, raw, x, table, rows_a, rows_b, 0, points // LANES // 2)

    @pl.when(rep == 0)
    def _():
        share_basis()

    gather(order, raw, x, table, rows_a, rows_b, points // LANES // 2, points // LANES)

    def chunk(i):
        return pl.ds(pl.multiple_of(i * CHUNK, CHUNK), CHUNK)

    steps = points // CHUNK

    def wait_basis(n):
        for copy in basis_copies[n]:
            copy.wait()

    wait_basis(0)
    local = levels[0][2]
    per_node = steps // local
    sums = []
    for node in range(local):
        def first_step(i, total):
            return total + dot_nt(x[:, chunk(i)], basis[0, :, chunk(i)])

        sums.append(
            lax.fori_loop(
                node * per_node, (node + 1) * per_node, first_step, jnp.zeros((rhs, RANK), F32)
            )
        )

    for n, (level, span, local, stages, factor) in enumerate(levels):
        for copy in cap_copies[n]:
            copy.wait()
        if local > 1:
            s = jnp.concatenate(sums, axis=1)
            c = caps[n]
        else:
            total = sums[0]
            sibling = None
            c = caps[n, 0:RANK, :]
            for stage in stages:
                slot0 = stage[0][2]
                send[slot0] = total.astype(BF16)
                copies = []
                for mask, crosses, slot in stage:
                    copy = pltpu.make_async_remote_copy(
                        src_ref=send.at[slot0],
                        dst_ref=recv.at[slot],
                        send_sem=send_sems.at[slot],
                        recv_sem=recv_sems.at[slot],
                        device_id=partner(mask),
                        device_id_type=MESH,
                    )
                    copy.start()
                    copies.append(copy)
                for copy, (mask, crosses, slot) in zip(copies, stage):
                    copy.wait()
                    value = recv[slot].astype(F32)
                    if crosses:
                        sibling = value if sibling is None else sibling + value
                    else:
                        total = total + value
            s = jnp.concatenate([total, sibling], axis=1)
        c_high, c_low = split(c)
        s_high, s_low = split(s)
        coefficients = dot_nt(s_high, c_high) + dot_nt(s_low, c_high) + dot_nt(s_high, c_low)
        coefficients = (coefficients * factor).astype(BF16)
        before = x if n == 0 else current
        last = n == LEVELS - 1
        if not last:
            wait_basis(n + 1)
            next_local = levels[n + 1][2]
        pieces = max(local, 1 if last else next_local)
        width = steps // pieces
        sums = []
        for piece in range(pieces):
            node = piece * local // pieces
            mine = coefficients[:, node * RANK : (node + 1) * RANK]

            def step(i, total):
                here = chunk(i)
                update = jnp.dot(mine, basis[n, :, here], preferred_element_type=F32)
                value = before[:, here].astype(F32) - update
                if last:
                    result[:, here] = value.astype(BF16)
                    return total
                current[:, here] = value
                return total + dot_nt(value.astype(BF16), basis[n + 1, :, here])

            if last:
                out_copies = []
                for part in range(PIECES):
                    for i in range(part * steps // PIECES, (part + 1) * steps // PIECES):
                        step(i, None)
                    cols = pl.ds(part * piece_width, piece_width)
                    out_copies.append(
                        pltpu.make_async_copy(result.at[:, cols], out.at[:, cols], out_sems.at[part])
                    )
                    out_copies[-1].start()
                for copy in out_copies:
                    copy.wait()
                return
            total = lax.fori_loop(
                piece * width, (piece + 1) * width, step, jnp.zeros((rhs, RANK), F32)
            )
            sums.append(total)
        group = pieces // next_local
        sums = [sum(sums[i * group + 1 : (i + 1) * group], sums[i * group]) for i in range(next_local)]


def shards(right_sides, curve_order, level_bases, capacitance):
    rhs, points = right_sides.shape
    total = points * lax.axis_size(("pts", "sub"))
    levels, slots = plan(points, total)
    hbm = pl.BlockSpec(memory_space=pltpu.MemorySpace.HBM)
    return pl.pallas_call(
        functools.partial(solve_kernel, levels),
        out_shape=jax.ShapeDtypeStruct((rhs, points), BF16),
        in_specs=[hbm, hbm, hbm, hbm],
        out_specs=hbm,
        scratch_shapes=[
            pltpu.VMEM((rhs, points), BF16),
            pltpu.SMEM((1, points), jnp.int32),
            pltpu.VMEM((rhs, points), BF16),
            pltpu.VMEM((points, LANES), F32),
            pltpu.VMEM((LANES, LANES), F32),
            pltpu.VMEM((LANES, LANES), F32),
            pltpu.VMEM((rhs, points), F32),
            pltpu.VMEM((LEVELS, RANK, points), BF16),
            pltpu.VMEM((LEVELS, 2 * RANK, 2 * RANK), F32),
            pltpu.VMEM((rhs, points), BF16),
            pltpu.VMEM((slots, rhs, RANK), BF16),
            pltpu.VMEM((slots, rhs, RANK), BF16),
            pltpu.SemaphoreType.DMA((PIECES + 1,)),
            pltpu.SemaphoreType.DMA((LEVELS,)),
            pltpu.SemaphoreType.DMA((LEVELS,)),
            pltpu.SemaphoreType.DMA((LEVELS,)),
            pltpu.SemaphoreType.DMA((LEVELS, 2)),
            pltpu.SemaphoreType.DMA((PIECES,)),
            pltpu.SemaphoreType.DMA((slots,)),
            pltpu.SemaphoreType.DMA((slots,)),
        ],
        compiler_params=pltpu.CompilerParams(
            collective_id=0, has_side_effects=True, vmem_limit_bytes=62 * 2**20
        ),
        cost_estimate=pl.CostEstimate(
            flops=16 * rhs * RANK * points, bytes_accessed=20 * 2**20, transcendentals=0
        ),
        name="tree_solve",
    )(right_sides, curve_order, level_bases, capacitance)


def solution(mesh):
    in_specs = (
        P("rep", ("cls", "pts", "sub")),
        P(("cls", "pts", "sub"), None),
        P(None, "rep", ("cls", "pts", "sub")),
        P("cls", None, None),
    )
    out_specs = P("rep", ("cls", "pts", "sub"))
    return jax.shard_map(shards, mesh=mesh, in_specs=in_specs, out_specs=out_specs, check_vma=False)
```

```python
import functools
import math

import jax
import jax.numpy as jnp
from jax import lax
from jax.experimental import pallas as pl
from jax.experimental.pallas import tpu as pltpu
from jax.sharding import PartitionSpec as P

RANK = 128
LEVELS = 4
LANES = 128
CHUNK = 1024
PIECES = 4
STAGE_BITS = 2
MESH = pl.DeviceIdType.MESH
F32 = jnp.float32
BF16 = jnp.bfloat16


def dot_nt(a, b):
    return lax.dot_general(a, b, (((1,), (1,)), ((), ())), preferred_element_type=F32)


def plan(points, total):
    levels, slot = [], 0
    for level in range(LEVELS, 0, -1):
        size = total // 2**level
        span, local = max(size // points, 1), max(points // size, 1)
        stages = []
        if local == 1:
            sibling = span.bit_length() - 1
            bits = list(range(sibling + 1))
            for at in range(0, len(bits), STAGE_BITS):
                group = bits[at : at + STAGE_BITS]
                masks = []
                for mix in range(1, 2 ** len(group)):
                    mask = sum(1 << bit for i, bit in enumerate(group) if mix >> i & 1)
                    masks.append((mask, bool(mask >> sibling & 1), slot))
                    slot += 1
                stages.append(masks)
        factor = 0.3 * 2**level * math.sqrt(size / RANK)
        levels.append((level, span, local, stages, factor))
    return levels, slot


def split(value):
    high = value.astype(BF16)
    return high, (value - high.astype(F32)).astype(BF16)


def gather(order, x, out, table, rows_a, rows_b, first, stop):
    rhs = x.shape[0]

    def pick(b, rows):
        for j in range(LANES):
            rows[pl.ds(j, 1), :] = table[pl.ds(order[0, b * LANES + j], 1), :]

    def put(b, rows):
        cols = pl.ds(pl.multiple_of(b * LANES, LANES), LANES)
        out[:, cols] = rows[...].astype(BF16).T[0:rhs]

    pick(first, rows_a)

    @pl.loop(first // 2, stop // 2 - 1)
    def _(i):
        pick(2 * i + 1, rows_b)
        put(2 * i, rows_a)
        pick(2 * i + 2, rows_a)
        put(2 * i + 1, rows_b)

    pick(stop - 1, rows_b)
    put(stop - 2, rows_a)
    put(stop - 1, rows_b)


def solve_kernel(
    levels, sides, order_in, own, cap, out,
    raw, order, x, table, rows_a, rows_b, current, basis, caps, send, recv,
    in_sems, basis_sems, far_send_sems, far_recv_sems, cap_sems, send_sems, recv_sems,
):
    rhs, points = raw.shape
    half = own.shape[1]
    sub_size = lax.axis_size("sub")
    sub_bits = sub_size.bit_length() - 1
    pts, sub = lax.axis_index("pts"), lax.axis_index("sub")
    rep = lax.axis_index("rep")
    block = pts * sub_size + sub

    def partner(mask):
        def flip(value, bits):
            for i in range(bits.bit_length()):
                if bits >> i & 1:
                    value = value + (1 << i) * (1 - 2 * (value // (1 << i) % 2))
            return value

        return {"pts": flip(pts, mask >> sub_bits), "sub": flip(sub, mask & sub_size - 1)}

    masks = sorted({m for _, _, _, stages, _ in levels for stage in stages for m, _, _ in stage})
    barrier = pltpu.get_barrier_semaphore()
    pl.semaphore_signal(barrier, inc=1, device_id={"rep": 1 - rep}, device_id_type=MESH)
    for mask in masks:
        pl.semaphore_signal(barrier, inc=1, device_id=partner(mask), device_id_type=MESH)

    piece_width = points // PIECES
    side_copies = []
    for piece in range(PIECES):
        cols = pl.ds(piece * piece_width, piece_width)
        side_copies.append(
            pltpu.make_async_copy(sides.at[:, cols], raw.at[:, cols], in_sems.at[piece])
        )
        side_copies[-1].start()
    order_copy = pltpu.make_async_copy(order_in, order, in_sems.at[PIECES])
    order_copy.start()

    basis_copies, cap_copies = [], []
    for n, (level, span, local, _, _) in enumerate(levels):
        first = block // span * local
        parent = 2 ** (level - 1) - 1 + first // 2
        odd = first % 2
        mine_at = basis.at[n, pl.ds(pl.multiple_of(rep * half, half), half), :]
        here = pltpu.make_async_copy(own.at[level - 1], mine_at, basis_sems.at[n])
        far = pltpu.make_async_remote_copy(
            src_ref=own.at[level - 1],
            dst_ref=mine_at,
            send_sem=far_send_sems.at[n],
            recv_sem=far_recv_sems.at[n],
            device_id={"rep": 1 - rep},
            device_id_type=MESH,
        )
        basis_copies.append((here, far))
        if local == 1:
            mine = pl.ds(pl.multiple_of(odd * RANK, RANK), RANK)
            theirs = pl.ds(pl.multiple_of((1 - odd) * RANK, RANK), RANK)
            cap_copies.append(
                [
                    pltpu.make_async_copy(
                        cap.at[parent, mine, cols],
                        caps.at[n, 0:RANK, piece * RANK : (piece + 1) * RANK],
                        cap_sems.at[n, piece],
                    )
                    for piece, cols in enumerate((mine, theirs))
                ]
            )
        else:
            cap_copies.append([pltpu.make_async_copy(cap.at[parent], caps.at[n], cap_sems.at[n, 0])])
        for copy in [here] + cap_copies[-1]:
            copy.start()

    def share_basis():
        pl.semaphore_wait(barrier, len(masks) + 1)
        for _, far in basis_copies:
            far.start()

    @pl.when(rep != 0)
    def _():
        share_basis()

    for piece in range(PIECES):
        side_copies[piece].wait()

        @pl.loop(piece * piece_width // LANES, (piece + 1) * piece_width // LANES, unroll=4)
        def _(b):
            cols = pl.ds(pl.multiple_of(b * LANES, LANES), LANES)
            table[cols, 0:rhs] = raw[:, cols].T.astype(F32)

    order_copy.wait()
    gather(order, raw, x, table, rows_a, rows_b, 0, points // LANES // 2)

    @pl.when(rep == 0)
    def _():
        share_basis()

    gather(order, raw, x, table, rows_a, rows_b, points // LANES // 2, points // LANES)

    def chunk(i):
        return pl.ds(pl.multiple_of(i * CHUNK, CHUNK), CHUNK)

    steps = points // CHUNK

    def wait_basis(n):
        for copy in basis_copies[n]:
            copy.wait()

    wait_basis(0)
    local = levels[0][2]
    per_node = steps // local
    sums = []
    for node in range(local):
        def first_step(i, total):
            return total + dot_nt(x[:, chunk(i)], basis[0, :, chunk(i)])

        sums.append(
            lax.fori_loop(
                node * per_node, (node + 1) * per_node, first_step, jnp.zeros((rhs, RANK), F32)
            )
        )

    def sweep(n, source, pending):
        ahead = n + 1 < LEVELS
        if ahead:
            wait_basis(n + 1)

        def step(i, total):
            here = chunk(i)
            value = source[:, here]
            if pending is not None:
                value = value - jnp.dot(
                    pending, basis[n - 1, :, here], preferred_element_type=F32
                )
                current[:, here] = value
            if not ahead:
                return total
            left = jnp.concatenate([value.astype(BF16), basis[n, :, here]], axis=0)
            return total + dot_nt(left, basis[n + 1, :, here])

        return lax.fori_loop(0, steps, step, jnp.zeros((rhs + RANK, RANK), F32))

    source, pending = x, None
    for n, (level, span, local, stages, factor) in enumerate(levels):
        last = n == LEVELS - 1
        for copy in cap_copies[n]:
            copy.wait()
        if local > 1:
            s = jnp.concatenate(sums, axis=1)
            c = caps[n]
        else:
            total = sums[0]
            sibling = None
            c = caps[n, 0:RANK, :]
            for at, stage in enumerate(stages):
                slot0 = stage[0][2]
                send[slot0] = total.astype(BF16)
                copies = []
                for mask, crosses, slot in stage:
                    copy = pltpu.make_async_remote_copy(
                        src_ref=send.at[slot0],
                        dst_ref=recv.at[slot],
                        send_sem=send_sems.at[slot],
                        recv_sem=recv_sems.at[slot],
                        device_id=partner(mask),
                        device_id_type=MESH,
                    )
                    copy.start()
                    copies.append(copy)
                if at == 0:
                    products = sweep(n, source, pending)
                    if pending is not None:
                        source = current
                for copy, (mask, crosses, slot) in zip(copies, stage):
                    copy.wait()
                    value = recv[slot].astype(F32)
                    if crosses:
                        sibling = value if sibling is None else sibling + value
                    else:
                        total = total + value
            s = jnp.concatenate([total, sibling], axis=1)
        c_high, c_low = split(c)
        s_high, s_low = split(s)
        coefficients = dot_nt(s_high, c_high) + dot_nt(s_low, c_high) + dot_nt(s_high, c_low)
        coefficients = (coefficients * factor).astype(BF16)
        if local == 1 and not last:
            g_high, g_low = split(products[rhs:])
            change = jnp.dot(coefficients, g_high, preferred_element_type=F32)
            change = change + jnp.dot(coefficients, g_low, preferred_element_type=F32)
            sums = [products[0:rhs] - change]
            pending = coefficients
            continue
        if local == 1:
            for i in range(steps):
                here = chunk(i)
                update = jnp.dot(coefficients, basis[n, :, here], preferred_element_type=F32)
                out[:, here] = (source[:, here].astype(F32) - update).astype(BF16)
            return
        wait_basis(n + 1)
        next_local = levels[n + 1][2]
        width = steps // local
        sums = []
        for node in range(local):
            mine = coefficients[:, node * RANK : (node + 1) * RANK]

            def step(i, total):
                here = chunk(i)
                update = jnp.dot(mine, basis[n, :, here], preferred_element_type=F32)
                value = source[:, here].astype(F32) - update
                current[:, here] = value
                return total + dot_nt(value.astype(BF16), basis[n + 1, :, here])

            sums.append(
                lax.fori_loop(node * width, (node + 1) * width, step, jnp.zeros((rhs, RANK), F32))
            )
        source = current
        group = local // next_local
        sums = [sum(sums[i * group + 1 : (i + 1) * group], sums[i * group]) for i in range(next_local)]


def shards(right_sides, curve_order, level_bases, capacitance):
    rhs, points = right_sides.shape
    total = points * lax.axis_size(("pts", "sub"))
    levels, slots = plan(points, total)
    hbm = pl.BlockSpec(memory_space=pltpu.MemorySpace.HBM)
    return pl.pallas_call(
        functools.partial(solve_kernel, levels),
        out_shape=jax.ShapeDtypeStruct((rhs, points), BF16),
        in_specs=[hbm, hbm, hbm, hbm],
        out_specs=pl.BlockSpec(memory_space=pltpu.VMEM),
        scratch_shapes=[
            pltpu.VMEM((rhs, points), BF16),
            pltpu.SMEM((1, points), jnp.int32),
            pltpu.VMEM((rhs, points), BF16),
            pltpu.VMEM((points, LANES), F32),
            pltpu.VMEM((LANES, LANES), F32),
            pltpu.VMEM((LANES, LANES), F32),
            pltpu.VMEM((rhs, points), F32),
            pltpu.VMEM((LEVELS, RANK, points), BF16),
            pltpu.VMEM((LEVELS, 2 * RANK, 2 * RANK), F32),
            pltpu.VMEM((slots, rhs, RANK), BF16),
            pltpu.VMEM((slots, rhs, RANK), BF16),
            pltpu.SemaphoreType.DMA((PIECES + 1,)),
            pltpu.SemaphoreType.DMA((LEVELS,)),
            pltpu.SemaphoreType.DMA((LEVELS,)),
            pltpu.SemaphoreType.DMA((LEVELS,)),
            pltpu.SemaphoreType.DMA((LEVELS, 2)),
            pltpu.SemaphoreType.DMA((slots,)),
            pltpu.SemaphoreType.DMA((slots,)),
        ],
        compiler_params=pltpu.CompilerParams(
            collective_id=0, has_side_effects=True, vmem_limit_bytes=61 * 2**20
        ),
        cost_estimate=pl.CostEstimate(
            flops=16 * rhs * RANK * points, bytes_accessed=20 * 2**20, transcendentals=0
        ),
        name="tree_solve",
    )(right_sides, curve_order, level_bases, capacitance)


def solution(mesh):
    in_specs = (
        P("rep", ("cls", "pts", "sub")),
        P(("cls", "pts", "sub"), None),
        P(None, "rep", ("cls", "pts", "sub")),
        P("cls", None, None),
    )
    out_specs = P("rep", ("cls", "pts", "sub"))
    return jax.shard_map(shards, mesh=mesh, in_specs=in_specs, out_specs=out_specs, check_vma=False)
```

```python
import functools
import math

import jax
import jax.numpy as jnp
from jax import lax
from jax.experimental import pallas as pl
from jax.experimental.pallas import tpu as pltpu
from jax.sharding import PartitionSpec as P

RANK = 128
LEVELS = 4
LANES = 128
CHUNK = 1024
PIECES = 4
STAGE_BITS = 2
MESH = pl.DeviceIdType.MESH
F32 = jnp.float32
BF16 = jnp.bfloat16


def dot_nt(a, b):
    return lax.dot_general(a, b, (((1,), (1,)), ((), ())), preferred_element_type=F32)


def plan(points, total):
    levels, slot = [], 0
    for level in range(LEVELS, 0, -1):
        size = total // 2**level
        span, local = max(size // points, 1), max(points // size, 1)
        stages = []
        if local == 1:
            sibling = span.bit_length() - 1
            bits = list(range(sibling + 1))
            for at in range(0, len(bits), STAGE_BITS):
                group = bits[at : at + STAGE_BITS]
                masks = []
                for mix in range(1, 2 ** len(group)):
                    mask = sum(1 << bit for i, bit in enumerate(group) if mix >> i & 1)
                    masks.append((mask, bool(mask >> sibling & 1), slot))
                    slot += 1
                stages.append(masks)
        factor = 0.3 * 2**level * math.sqrt(size / RANK)
        levels.append((level, span, local, stages, factor))
    return levels, slot


def split(value):
    high = value.astype(BF16)
    return high, (value - high.astype(F32)).astype(BF16)


def gather(order, x, out, table, rows_a, rows_b, first, stop):
    rhs = x.shape[0]

    table_rows = table.reshape(table.shape[0], 1, LANES)

    def pick(b, rows):
        picked = rows.reshape(LANES, 1, LANES)
        for j in range(LANES):
            picked[j] = table_rows[order[0, b * LANES + j]]

    def put(b, rows):
        cols = pl.ds(pl.multiple_of(b * LANES, LANES), LANES)
        out[:, cols] = rows[...].astype(BF16).T[0:rhs]

    pick(first, rows_a)

    @pl.loop(first // 2, stop // 2 - 1)
    def _(i):
        pick(2 * i + 1, rows_b)
        put(2 * i, rows_a)
        pick(2 * i + 2, rows_a)
        put(2 * i + 1, rows_b)

    pick(stop - 1, rows_b)
    put(stop - 2, rows_a)
    put(stop - 1, rows_b)


def solve_kernel(
    levels, sides, order_in, own, cap, out,
    raw, order, x, table, rows_a, rows_b, current, basis, caps, send, recv,
    in_sems, basis_sems, far_send_sems, far_recv_sems, cap_sems, send_sems, recv_sems,
):
    rhs, points = raw.shape
    half = own.shape[1]
    sub_size = lax.axis_size("sub")
    sub_bits = sub_size.bit_length() - 1
    pts, sub = lax.axis_index("pts"), lax.axis_index("sub")
    rep = lax.axis_index("rep")
    block = pts * sub_size + sub

    def partner(mask):
        def flip(value, bits):
            for i in range(bits.bit_length()):
                if bits >> i & 1:
                    value = value + (1 << i) * (1 - 2 * (value // (1 << i) % 2))
            return value

        return {"pts": flip(pts, mask >> sub_bits), "sub": flip(sub, mask & sub_size - 1)}

    masks = sorted({m for _, _, _, stages, _ in levels for stage in stages for m, _, _ in stage})
    barrier = pltpu.get_barrier_semaphore()
    pl.semaphore_signal(barrier, inc=1, device_id={"rep": 1 - rep}, device_id_type=MESH)
    for mask in masks:
        pl.semaphore_signal(barrier, inc=1, device_id=partner(mask), device_id_type=MESH)

    piece_width = points // PIECES
    side_copies = []
    for piece in range(PIECES):
        cols = pl.ds(piece * piece_width, piece_width)
        side_copies.append(
            pltpu.make_async_copy(sides.at[:, cols], raw.at[:, cols], in_sems.at[piece])
        )
        side_copies[-1].start()
    order_copy = pltpu.make_async_copy(order_in, order, in_sems.at[PIECES])
    order_copy.start()

    basis_copies, cap_copies = [], []
    for n, (level, span, local, _, _) in enumerate(levels):
        first = block // span * local
        parent = 2 ** (level - 1) - 1 + first // 2
        odd = first % 2
        mine_at = basis.at[n, pl.ds(pl.multiple_of(rep * half, half), half), :]
        here = pltpu.make_async_copy(own.at[level - 1], mine_at, basis_sems.at[n])
        far = pltpu.make_async_remote_copy(
            src_ref=own.at[level - 1],
            dst_ref=mine_at,
            send_sem=far_send_sems.at[n],
            recv_sem=far_recv_sems.at[n],
            device_id={"rep": 1 - rep},
            device_id_type=MESH,
        )
        basis_copies.append((here, far))
        if local == 1:
            mine = pl.ds(pl.multiple_of(odd * RANK, RANK), RANK)
            theirs = pl.ds(pl.multiple_of((1 - odd) * RANK, RANK), RANK)
            cap_copies.append(
                [
                    pltpu.make_async_copy(
                        cap.at[parent, mine, cols],
                        caps.at[n, 0:RANK, piece * RANK : (piece + 1) * RANK],
                        cap_sems.at[n, piece],
                    )
                    for piece, cols in enumerate((mine, theirs))
                ]
            )
        else:
            cap_copies.append([pltpu.make_async_copy(cap.at[parent], caps.at[n], cap_sems.at[n, 0])])
        for copy in [here] + cap_copies[-1]:
            copy.start()

    def share_basis():
        pl.semaphore_wait(barrier, len(masks) + 1)
        for _, far in basis_copies:
            far.start()

    @pl.when(rep != 0)
    def _():
        share_basis()

    for piece in range(PIECES):
        side_copies[piece].wait()

        @pl.loop(piece * piece_width // LANES, (piece + 1) * piece_width // LANES, unroll=4)
        def _(b):
            cols = pl.ds(pl.multiple_of(b * LANES, LANES), LANES)
            table[cols, 0:rhs] = raw[:, cols].T.astype(F32)

    order_copy.wait()
    gather(order, raw, x, table, rows_a, rows_b, 0, points // LANES // 2)

    @pl.when(rep == 0)
    def _():
        share_basis()

    gather(order, raw, x, table, rows_a, rows_b, points // LANES // 2, points // LANES)

    def chunk(i):
        return pl.ds(pl.multiple_of(i * CHUNK, CHUNK), CHUNK)

    steps = points // CHUNK

    def wait_basis(n):
        for copy in basis_copies[n]:
            copy.wait()

    wait_basis(0)
    local = levels[0][2]
    per_node = steps // local
    sums = []
    for node in range(local):
        def first_step(i, total):
            return total + dot_nt(x[:, chunk(i)], basis[0, :, chunk(i)])

        sums.append(
            lax.fori_loop(
                node * per_node, (node + 1) * per_node, first_step, jnp.zeros((rhs, RANK), F32)
            )
        )

    def sweep(n, source, pending):
        ahead = n + 1 < LEVELS
        if ahead:
            wait_basis(n + 1)

        def step(i, total):
            here = chunk(i)
            value = source[:, here]
            if pending is not None:
                value = value - jnp.dot(
                    pending, basis[n - 1, :, here], preferred_element_type=F32
                )
                current[:, here] = value
            if not ahead:
                return total
            left = jnp.concatenate([value.astype(BF16), basis[n, :, here]], axis=0)
            return total + dot_nt(left, basis[n + 1, :, here])

        return lax.fori_loop(0, steps, step, jnp.zeros((rhs + RANK, RANK), F32))

    source, pending = x, None
    for n, (level, span, local, stages, factor) in enumerate(levels):
        last = n == LEVELS - 1
        for copy in cap_copies[n]:
            copy.wait()
        if local > 1:
            s = jnp.concatenate(sums, axis=1)
            c = caps[n]
        else:
            total = sums[0]
            sibling = None
            c = caps[n, 0:RANK, :]
            for at, stage in enumerate(stages):
                slot0 = stage[0][2]
                send[slot0] = total.astype(BF16)
                copies = []
                for mask, crosses, slot in stage:
                    copy = pltpu.make_async_remote_copy(
                        src_ref=send.at[slot0],
                        dst_ref=recv.at[slot],
                        send_sem=send_sems.at[slot],
                        recv_sem=recv_sems.at[slot],
                        device_id=partner(mask),
                        device_id_type=MESH,
                    )
                    copy.start()
                    copies.append(copy)
                if at == 0:
                    products = sweep(n, source, pending)
                    if pending is not None:
                        source = current
                for copy, (mask, crosses, slot) in zip(copies, stage):
                    copy.wait()
                    value = recv[slot].astype(F32)
                    if crosses:
                        sibling = value if sibling is None else sibling + value
                    else:
                        total = total + value
            s = jnp.concatenate([total, sibling], axis=1)
        c_high, c_low = split(c)
        s_high, s_low = split(s)
        coefficients = dot_nt(s_high, c_high) + dot_nt(s_low, c_high) + dot_nt(s_high, c_low)
        coefficients = (coefficients * factor).astype(BF16)
        if local == 1 and not last:
            g_high, g_low = split(products[rhs:])
            change = jnp.dot(coefficients, g_high, preferred_element_type=F32)
            change = change + jnp.dot(coefficients, g_low, preferred_element_type=F32)
            sums = [products[0:rhs] - change]
            pending = coefficients
            continue
        if local == 1:
            for i in range(steps):
                here = chunk(i)
                update = jnp.dot(coefficients, basis[n, :, here], preferred_element_type=F32)
                out[:, here] = (source[:, here].astype(F32) - update).astype(BF16)
            return
        wait_basis(n + 1)
        next_local = levels[n + 1][2]
        width = steps // local
        sums = []
        for node in range(local):
            mine = coefficients[:, node * RANK : (node + 1) * RANK]

            def step(i, total):
                here = chunk(i)
                update = jnp.dot(mine, basis[n, :, here], preferred_element_type=F32)
                value = source[:, here].astype(F32) - update
                current[:, here] = value
                return total + dot_nt(value.astype(BF16), basis[n + 1, :, here])

            sums.append(
                lax.fori_loop(node * width, (node + 1) * width, step, jnp.zeros((rhs, RANK), F32))
            )
        source = current
        group = local // next_local
        sums = [sum(sums[i * group + 1 : (i + 1) * group], sums[i * group]) for i in range(next_local)]


def shards(right_sides, curve_order, level_bases, capacitance):
    rhs, points = right_sides.shape
    total = points * lax.axis_size(("pts", "sub"))
    levels, slots = plan(points, total)
    hbm = pl.BlockSpec(memory_space=pltpu.MemorySpace.HBM)
    return pl.pallas_call(
        functools.partial(solve_kernel, levels),
        out_shape=jax.ShapeDtypeStruct((rhs, points), BF16),
        in_specs=[hbm, hbm, hbm, hbm],
        out_specs=pl.BlockSpec(memory_space=pltpu.VMEM),
        scratch_shapes=[
            pltpu.VMEM((rhs, points), BF16),
            pltpu.SMEM((1, points), jnp.int32),
            pltpu.VMEM((rhs, points), BF16),
            pltpu.VMEM((points, LANES), F32),
            pltpu.VMEM((LANES, LANES), F32),
            pltpu.VMEM((LANES, LANES), F32),
            pltpu.VMEM((rhs, points), F32),
            pltpu.VMEM((LEVELS, RANK, points), BF16),
            pltpu.VMEM((LEVELS, 2 * RANK, 2 * RANK), F32),
            pltpu.VMEM((slots, rhs, RANK), BF16),
            pltpu.VMEM((slots, rhs, RANK), BF16),
            pltpu.SemaphoreType.DMA((PIECES + 1,)),
            pltpu.SemaphoreType.DMA((LEVELS,)),
            pltpu.SemaphoreType.DMA((LEVELS,)),
            pltpu.SemaphoreType.DMA((LEVELS,)),
            pltpu.SemaphoreType.DMA((LEVELS, 2)),
            pltpu.SemaphoreType.DMA((slots,)),
            pltpu.SemaphoreType.DMA((slots,)),
        ],
        compiler_params=pltpu.CompilerParams(
            collective_id=0, has_side_effects=True, vmem_limit_bytes=60 * 2**20
        ),
        cost_estimate=pl.CostEstimate(
            flops=16 * rhs * RANK * points, bytes_accessed=20 * 2**20, transcendentals=0
        ),
        name="tree_solve",
    )(right_sides, curve_order, level_bases, capacitance)


def solution(mesh):
    in_specs = (
        P("rep", ("cls", "pts", "sub")),
        P(("cls", "pts", "sub"), None),
        P(None, "rep", ("cls", "pts", "sub")),
        P("cls", None, None),
    )
    out_specs = P("rep", ("cls", "pts", "sub"))
    return jax.shard_map(shards, mesh=mesh, in_specs=in_specs, out_specs=out_specs, check_vma=False)
```

```python
import functools
import math

import jax
import jax.numpy as jnp
from jax import lax
from jax.experimental import pallas as pl
from jax.experimental.pallas import tpu as pltpu
from jax.sharding import PartitionSpec as P

RANK = 128
LEVELS = 4
LANES = 128
CHUNK = 1024
PIECES = 4
STAGE_BITS = 2
MESH = pl.DeviceIdType.MESH
F32 = jnp.float32
BF16 = jnp.bfloat16


def dot_nt(a, b):
    return lax.dot_general(a, b, (((1,), (1,)), ((), ())), preferred_element_type=F32)


def plan(points, total):
    levels, slot = [], 0
    for level in range(LEVELS, 0, -1):
        size = total // 2**level
        span, local = max(size // points, 1), max(points // size, 1)
        stages = []
        if local == 1:
            sibling = span.bit_length() - 1
            bits = list(range(sibling + 1))
            for at in range(0, len(bits), STAGE_BITS):
                group = bits[at : at + STAGE_BITS]
                masks = []
                for mix in range(1, 2 ** len(group)):
                    mask = sum(1 << bit for i, bit in enumerate(group) if mix >> i & 1)
                    masks.append((mask, bool(mask >> sibling & 1), slot))
                    slot += 1
                stages.append(masks)
        factor = 0.3 * 2**level * math.sqrt(size / RANK)
        levels.append((level, span, local, stages, factor))
    return levels, slot


def split(value):
    high = value.astype(BF16)
    return high, (value - high.astype(F32)).astype(BF16)


def gather(order, x, out, table, rows_a, rows_b, first, stop, beside=None, carry=None):
    rhs = x.shape[0]

    table_rows = table.reshape(table.shape[0], 1, LANES)

    def pick(b, rows):
        picked = rows.reshape(LANES, 1, LANES)
        for j in range(LANES):
            picked[j] = table_rows[order[0, b * LANES + j]]

    def put(b, rows):
        cols = pl.ds(pl.multiple_of(b * LANES, LANES), LANES)
        out[:, cols] = rows[...].astype(BF16).T[0:rhs]

    pick(first, rows_a)

    def step(i, carry):
        pick(2 * i + 1, rows_b)
        put(2 * i, rows_a)
        if beside is not None:
            carry = beside(i - first // 2, carry)
        pick(2 * i + 2, rows_a)
        put(2 * i + 1, rows_b)
        return carry

    carry = lax.fori_loop(first // 2, stop // 2 - 1, step, carry)
    pick(stop - 1, rows_b)
    put(stop - 2, rows_a)
    if beside is not None:
        carry = beside((stop - first) // 2 - 1, carry)
    put(stop - 1, rows_b)
    return carry


def solve_kernel(
    levels, sides, order_in, own, cap, out,
    raw, order, x, table, rows_a, rows_b, current, basis, caps, send, recv,
    in_sems, basis_sems, far_send_sems, far_recv_sems, cap_sems, send_sems, recv_sems,
):
    rhs, points = raw.shape
    half = own.shape[1]
    sub_size = lax.axis_size("sub")
    sub_bits = sub_size.bit_length() - 1
    pts, sub = lax.axis_index("pts"), lax.axis_index("sub")
    rep = lax.axis_index("rep")
    block = pts * sub_size + sub

    def partner(mask):
        def flip(value, bits):
            for i in range(bits.bit_length()):
                if bits >> i & 1:
                    value = value + (1 << i) * (1 - 2 * (value // (1 << i) % 2))
            return value

        return {"pts": flip(pts, mask >> sub_bits), "sub": flip(sub, mask & sub_size - 1)}

    masks = sorted({m for _, _, _, stages, _ in levels for stage in stages for m, _, _ in stage})
    barrier = pltpu.get_barrier_semaphore()
    pl.semaphore_signal(barrier, inc=1, device_id={"rep": 1 - rep}, device_id_type=MESH)
    for mask in masks:
        pl.semaphore_signal(barrier, inc=1, device_id=partner(mask), device_id_type=MESH)

    piece_width = points // PIECES
    side_copies = []
    for piece in range(PIECES):
        cols = pl.ds(piece * piece_width, piece_width)
        side_copies.append(
            pltpu.make_async_copy(sides.at[:, cols], raw.at[:, cols], in_sems.at[piece])
        )
        side_copies[-1].start()
    order_copy = pltpu.make_async_copy(order_in, order, in_sems.at[PIECES])
    order_copy.start()

    basis_copies, cap_copies = [], []
    for n, (level, span, local, _, _) in enumerate(levels):
        first = block // span * local
        parent = 2 ** (level - 1) - 1 + first // 2
        odd = first % 2
        mine_at = basis.at[n, pl.ds(pl.multiple_of(rep * half, half), half), :]
        here = pltpu.make_async_copy(own.at[level - 1], mine_at, basis_sems.at[n])
        far = pltpu.make_async_remote_copy(
            src_ref=own.at[level - 1],
            dst_ref=mine_at,
            send_sem=far_send_sems.at[n],
            recv_sem=far_recv_sems.at[n],
            device_id={"rep": 1 - rep},
            device_id_type=MESH,
        )
        basis_copies.append((here, far))
        if local == 1:
            mine = pl.ds(pl.multiple_of(odd * RANK, RANK), RANK)
            theirs = pl.ds(pl.multiple_of((1 - odd) * RANK, RANK), RANK)
            cap_copies.append(
                [
                    pltpu.make_async_copy(
                        cap.at[parent, mine, cols],
                        caps.at[n, 0:RANK, piece * RANK : (piece + 1) * RANK],
                        cap_sems.at[n, piece],
                    )
                    for piece, cols in enumerate((mine, theirs))
                ]
            )
        else:
            cap_copies.append([pltpu.make_async_copy(cap.at[parent], caps.at[n], cap_sems.at[n, 0])])
        for copy in [here] + cap_copies[-1]:
            copy.start()

    def share_basis():
        pl.semaphore_wait(barrier, len(masks) + 1)
        for _, far in basis_copies:
            far.start()

    @pl.when(rep != 0)
    def _():
        share_basis()

    for piece in range(PIECES):
        side_copies[piece].wait()

        @pl.loop(piece * piece_width // LANES, (piece + 1) * piece_width // LANES, unroll=4)
        def _(b):
            cols = pl.ds(pl.multiple_of(b * LANES, LANES), LANES)
            table[cols, 0:rhs] = raw[:, cols].T.astype(F32)

    order_copy.wait()
    def chunk(i):
        return pl.ds(pl.multiple_of(i * CHUNK, CHUNK), CHUNK)

    steps = points // CHUNK

    def wait_basis(n):
        for copy in basis_copies[n]:
            copy.wait()

    blocks = points // LANES
    local = levels[0][2]
    gather(order, raw, x, table, rows_a, rows_b, 0, blocks // 4)

    @pl.when(rep == 0)
    def _():
        share_basis()

    gather(order, raw, x, table, rows_a, rows_b, blocks // 4, blocks // 2)
    wait_basis(0)

    pair = 2 * LANES
    near = points // 2

    def project(at, total):
        cols = pl.ds(pl.multiple_of(at, pair), pair)
        return total + dot_nt(x[:, cols], basis[0, :, cols])

    def beside(i, totals):
        low, high = totals
        low = project(i * pair, low)
        before = near + i * pair - pair
        cols = pl.ds(pl.multiple_of(before, pair), pair)
        term = dot_nt(x[:, cols], basis[0, :, cols])
        return low, high + jnp.where(i > 0, term, 0.0)

    zero = jnp.zeros((rhs, RANK), F32)
    low, high = gather(
        order, raw, x, table, rows_a, rows_b, blocks // 2, blocks, beside, (zero, zero)
    )
    high = project(points - pair, high)
    sums = [low, high] if local > 1 else [low + high]

    def sweep(n, source, pending):
        ahead = n + 1 < LEVELS
        if ahead:
            wait_basis(n + 1)

        def step(i, total):
            here = chunk(i)
            value = source[:, here]
            if pending is not None:
                value = value - jnp.dot(
                    pending, basis[n - 1, :, here], preferred_element_type=F32
                )
                current[:, here] = value
            if not ahead:
                return total
            left = jnp.concatenate([value.astype(BF16), basis[n, :, here]], axis=0)
            return total + dot_nt(left, basis[n + 1, :, here])

        return lax.fori_loop(0, steps, step, jnp.zeros((rhs + RANK, RANK), F32))

    source, pending = x, None
    for n, (level, span, local, stages, factor) in enumerate(levels):
        last = n == LEVELS - 1
        for copy in cap_copies[n]:
            copy.wait()
        if local > 1:
            s = jnp.concatenate(sums, axis=1)
            c = caps[n]
        else:
            total = sums[0]
            sibling = None
            c = caps[n, 0:RANK, :]
            for at, stage in enumerate(stages):
                slot0 = stage[0][2]
                send[slot0] = total.astype(BF16)
                copies = []
                for mask, crosses, slot in stage:
                    copy = pltpu.make_async_remote_copy(
                        src_ref=send.at[slot0],
                        dst_ref=recv.at[slot],
                        send_sem=send_sems.at[slot],
                        recv_sem=recv_sems.at[slot],
                        device_id=partner(mask),
                        device_id_type=MESH,
                    )
                    copy.start()
                    copies.append(copy)
                if at == 0:
                    products = sweep(n, source, pending)
                    if pending is not None:
                        source = current
                for copy, (mask, crosses, slot) in zip(copies, stage):
                    copy.wait()
                    value = recv[slot].astype(F32)
                    if crosses:
                        sibling = value if sibling is None else sibling + value
                    else:
                        total = total + value
            s = jnp.concatenate([total, sibling], axis=1)
        c_high, c_low = split(c)
        s_high, s_low = split(s)
        coefficients = dot_nt(s_high, c_high) + dot_nt(s_low, c_high) + dot_nt(s_high, c_low)
        coefficients = (coefficients * factor).astype(BF16)
        if local == 1 and not last:
            g_high, g_low = split(products[rhs:])
            change = jnp.dot(coefficients, g_high, preferred_element_type=F32)
            change = change + jnp.dot(coefficients, g_low, preferred_element_type=F32)
            sums = [products[0:rhs] - change]
            pending = coefficients
            continue
        if local == 1:
            for i in range(steps):
                here = chunk(i)
                update = jnp.dot(coefficients, basis[n, :, here], preferred_element_type=F32)
                out[:, here] = (source[:, here].astype(F32) - update).astype(BF16)
            return
        wait_basis(n + 1)
        next_local = levels[n + 1][2]
        width = steps // local
        sums = []
        for node in range(local):
            mine = coefficients[:, node * RANK : (node + 1) * RANK]

            def step(i, total):
                here = chunk(i)
                update = jnp.dot(mine, basis[n, :, here], preferred_element_type=F32)
                value = source[:, here].astype(F32) - update
                current[:, here] = value
                return total + dot_nt(value.astype(BF16), basis[n + 1, :, here])

            sums.append(
                lax.fori_loop(node * width, (node + 1) * width, step, jnp.zeros((rhs, RANK), F32))
            )
        source = current
        group = local // next_local
        sums = [sum(sums[i * group + 1 : (i + 1) * group], sums[i * group]) for i in range(next_local)]


def shards(right_sides, curve_order, level_bases, capacitance):
    rhs, points = right_sides.shape
    total = points * lax.axis_size(("pts", "sub"))
    levels, slots = plan(points, total)
    hbm = pl.BlockSpec(memory_space=pltpu.MemorySpace.HBM)
    return pl.pallas_call(
        functools.partial(solve_kernel, levels),
        out_shape=jax.ShapeDtypeStruct((rhs, points), BF16),
        in_specs=[hbm, hbm, hbm, hbm],
        out_specs=pl.BlockSpec(memory_space=pltpu.VMEM),
        scratch_shapes=[
            pltpu.VMEM((rhs, points), BF16),
            pltpu.SMEM((1, points), jnp.int32),
            pltpu.VMEM((rhs, points), BF16),
            pltpu.VMEM((points, LANES), F32),
            pltpu.VMEM((LANES, LANES), F32),
            pltpu.VMEM((LANES, LANES), F32),
            pltpu.VMEM((rhs, points), F32),
            pltpu.VMEM((LEVELS, RANK, points), BF16),
            pltpu.VMEM((LEVELS, 2 * RANK, 2 * RANK), F32),
            pltpu.VMEM((slots, rhs, RANK), BF16),
            pltpu.VMEM((slots, rhs, RANK), BF16),
            pltpu.SemaphoreType.DMA((PIECES + 1,)),
            pltpu.SemaphoreType.DMA((LEVELS,)),
            pltpu.SemaphoreType.DMA((LEVELS,)),
            pltpu.SemaphoreType.DMA((LEVELS,)),
            pltpu.SemaphoreType.DMA((LEVELS, 2)),
            pltpu.SemaphoreType.DMA((slots,)),
            pltpu.SemaphoreType.DMA((slots,)),
        ],
        compiler_params=pltpu.CompilerParams(
            collective_id=0, has_side_effects=True, vmem_limit_bytes=58 * 2**20
        ),
        cost_estimate=pl.CostEstimate(
            flops=24 * rhs * RANK * points, bytes_accessed=16 * rhs * points, transcendentals=0
        ),
        name="tree_solve",
    )(right_sides, curve_order, level_bases, capacitance)


def solution(mesh):
    in_specs = (
        P("rep", ("cls", "pts", "sub")),
        P(("cls", "pts", "sub"), None),
        P(None, "rep", ("cls", "pts", "sub")),
        P("cls", None, None),
    )
    out_specs = P("rep", ("cls", "pts", "sub"))
    return jax.shard_map(shards, mesh=mesh, in_specs=in_specs, out_specs=out_specs, check_vma=False)
```

```python
import functools
import math

import jax
import jax.numpy as jnp
from jax import lax
from jax.experimental import pallas as pl
from jax.experimental.pallas import tpu as pltpu
from jax.sharding import PartitionSpec as P

RANK = 128
LEVELS = 4
LANES = 128
CHUNK = 1024
PIECES = 4
STAGE_BITS = 2
MESH = pl.DeviceIdType.MESH
F32 = jnp.float32
BF16 = jnp.bfloat16


def dot_nt(a, b):
    return lax.dot_general(a, b, (((1,), (1,)), ((), ())), preferred_element_type=F32)


def plan(points, total):
    levels, slot = [], 0
    for level in range(LEVELS, 0, -1):
        size = total // 2**level
        span, local = max(size // points, 1), max(points // size, 1)
        stages = []
        if local == 1:
            sibling = span.bit_length() - 1
            bits = list(range(sibling + 1))
            for at in range(0, len(bits), STAGE_BITS):
                group = bits[at : at + STAGE_BITS]
                masks = []
                for mix in range(1, 2 ** len(group)):
                    mask = sum(1 << bit for i, bit in enumerate(group) if mix >> i & 1)
                    masks.append((mask, bool(mask >> sibling & 1), slot))
                    slot += 1
                stages.append(masks)
        factor = 0.3 * 2**level * math.sqrt(size / RANK)
        levels.append((level, span, local, stages, factor))
    return levels, slot


def split(value):
    high = value.astype(BF16)
    return high, (value - high.astype(F32)).astype(BF16)


def gather(order, x, out, table, rows_a, rows_b, first, stop, beside=None, carry=None):
    rhs = x.shape[0]

    table_rows = table.reshape(table.shape[0], 1, LANES)

    def pick(b, rows):
        picked = rows.reshape(LANES, 1, LANES)
        for j in range(LANES):
            picked[j] = table_rows[order[0, b * LANES + j]]

    def put(b, rows):
        cols = pl.ds(pl.multiple_of(b * LANES, LANES), LANES)
        out[:, cols] = rows[...].astype(BF16).T[0:rhs]

    pick(first, rows_a)

    def step(i, carry):
        pick(2 * i + 1, rows_b)
        put(2 * i, rows_a)
        if beside is not None:
            carry = beside(i - first // 2, carry)
        pick(2 * i + 2, rows_a)
        put(2 * i + 1, rows_b)
        return carry

    carry = lax.fori_loop(first // 2, stop // 2 - 1, step, carry)
    pick(stop - 1, rows_b)
    put(stop - 2, rows_a)
    if beside is not None:
        carry = beside((stop - first) // 2 - 1, carry)
    put(stop - 1, rows_b)
    return carry


def solve_kernel(
    levels, sides, order_in, own, cap, out,
    raw, order, x, table, rows_a, rows_b, current, basis, caps, result, send, recv,
    in_sems, basis_sems, far_send_sems, far_recv_sems, cap_sems, out_sems, send_sems, recv_sems,
):
    rhs, points = raw.shape
    half = own.shape[1]
    sub_size = lax.axis_size("sub")
    sub_bits = sub_size.bit_length() - 1
    pts, sub = lax.axis_index("pts"), lax.axis_index("sub")
    rep = lax.axis_index("rep")
    block = pts * sub_size + sub

    def partner(mask):
        def flip(value, bits):
            for i in range(bits.bit_length()):
                if bits >> i & 1:
                    value = value + (1 << i) * (1 - 2 * (value // (1 << i) % 2))
            return value

        return {"pts": flip(pts, mask >> sub_bits), "sub": flip(sub, mask & sub_size - 1)}

    masks = sorted({m for _, _, _, stages, _ in levels for stage in stages for m, _, _ in stage})
    barrier = pltpu.get_barrier_semaphore()
    pl.semaphore_signal(barrier, inc=1, device_id={"rep": 1 - rep}, device_id_type=MESH)
    for mask in masks:
        pl.semaphore_signal(barrier, inc=1, device_id=partner(mask), device_id_type=MESH)

    piece_width = points // PIECES
    side_copies = []
    for piece in range(PIECES):
        cols = pl.ds(piece * piece_width, piece_width)
        side_copies.append(
            pltpu.make_async_copy(sides.at[:, cols], raw.at[:, cols], in_sems.at[piece])
        )
        side_copies[-1].start()
    order_copy = pltpu.make_async_copy(order_in, order, in_sems.at[PIECES])
    order_copy.start()

    basis_copies, cap_copies = [], []
    for n, (level, span, local, _, _) in enumerate(levels):
        first = block // span * local
        parent = 2 ** (level - 1) - 1 + first // 2
        odd = first % 2
        mine_at = basis.at[n, pl.ds(pl.multiple_of(rep * half, half), half), :]
        here = pltpu.make_async_copy(own.at[level - 1], mine_at, basis_sems.at[n])
        far = pltpu.make_async_remote_copy(
            src_ref=own.at[level - 1],
            dst_ref=mine_at,
            send_sem=far_send_sems.at[n],
            recv_sem=far_recv_sems.at[n],
            device_id={"rep": 1 - rep},
            device_id_type=MESH,
        )
        basis_copies.append((here, far))
        if local == 1:
            mine = pl.ds(pl.multiple_of(odd * RANK, RANK), RANK)
            theirs = pl.ds(pl.multiple_of((1 - odd) * RANK, RANK), RANK)
            cap_copies.append(
                [
                    pltpu.make_async_copy(
                        cap.at[parent, mine, cols],
                        caps.at[n, 0:RANK, piece * RANK : (piece + 1) * RANK],
                        cap_sems.at[n, piece],
                    )
                    for piece, cols in enumerate((mine, theirs))
                ]
            )
        else:
            cap_copies.append([pltpu.make_async_copy(cap.at[parent], caps.at[n], cap_sems.at[n, 0])])
        for copy in [here] + cap_copies[-1]:
            copy.start()

    def share_basis():
        pl.semaphore_wait(barrier, len(masks) + 1)
        for _, far in basis_copies:
            far.start()

    @pl.when(rep != 0)
    def _():
        share_basis()

    for piece in range(PIECES):
        side_copies[piece].wait()

        @pl.loop(piece * piece_width // LANES, (piece + 1) * piece_width // LANES, unroll=4)
        def _(b):
            cols = pl.ds(pl.multiple_of(b * LANES, LANES), LANES)
            table[cols, 0:rhs] = raw[:, cols].T.astype(F32)

    order_copy.wait()
    def chunk(i):
        return pl.ds(pl.multiple_of(i * CHUNK, CHUNK), CHUNK)

    steps = points // CHUNK

    def wait_basis(n):
        for copy in basis_copies[n]:
            copy.wait()

    blocks = points // LANES
    local = levels[0][2]
    gather(order, raw, x, table, rows_a, rows_b, 0, blocks // 4)

    @pl.when(rep == 0)
    def _():
        share_basis()

    gather(order, raw, x, table, rows_a, rows_b, blocks // 4, blocks // 2)
    wait_basis(0)

    pair = 2 * LANES
    near = points // 2

    def project(at, total):
        cols = pl.ds(pl.multiple_of(at, pair), pair)
        return total + dot_nt(x[:, cols], basis[0, :, cols])

    def beside(i, totals):
        low, high = totals
        low = project(i * pair, low)
        before = near + i * pair - pair
        cols = pl.ds(pl.multiple_of(before, pair), pair)
        term = dot_nt(x[:, cols], basis[0, :, cols])
        return low, high + jnp.where(i > 0, term, 0.0)

    zero = jnp.zeros((rhs, RANK), F32)
    low, high = gather(
        order, raw, x, table, rows_a, rows_b, blocks // 2, blocks, beside, (zero, zero)
    )
    high = project(points - pair, high)
    sums = [low, high] if local > 1 else [low + high]

    def sweep(n, source, pending):
        ahead = n + 1 < LEVELS
        if ahead:
            wait_basis(n + 1)

        def step(i, total):
            here = chunk(i)
            value = source[:, here]
            if pending is not None:
                value = value - jnp.dot(
                    pending, basis[n - 1, :, here], preferred_element_type=F32
                )
                current[:, here] = value
            if not ahead:
                return total
            left = jnp.concatenate([value.astype(BF16), basis[n, :, here]], axis=0)
            return total + dot_nt(left, basis[n + 1, :, here])

        return lax.fori_loop(0, steps, step, jnp.zeros((rhs + RANK, RANK), F32))

    source, pending = x, None
    for n, (level, span, local, stages, factor) in enumerate(levels):
        last = n == LEVELS - 1
        for copy in cap_copies[n]:
            copy.wait()
        if local > 1:
            s = jnp.concatenate(sums, axis=1)
            c_high, c_low = split(caps[n])
        else:
            total = sums[0]
            sibling = None
            for at, stage in enumerate(stages):
                slot0 = stage[0][2]
                send[slot0] = total.astype(BF16)
                copies = []
                for mask, crosses, slot in stage:
                    copy = pltpu.make_async_remote_copy(
                        src_ref=send.at[slot0],
                        dst_ref=recv.at[slot],
                        send_sem=send_sems.at[slot],
                        recv_sem=recv_sems.at[slot],
                        device_id=partner(mask),
                        device_id_type=MESH,
                    )
                    copy.start()
                    copies.append(copy)
                if at == 0:
                    products = sweep(n, source, pending)
                    if pending is not None:
                        source = current
                    c_high, c_low = split(caps[n, 0:RANK, :])
                    g_high, g_low = split(products[rhs:])
                for copy, (mask, crosses, slot) in zip(copies, stage):
                    copy.wait()
                    value = recv[slot].astype(F32)
                    if crosses:
                        sibling = value if sibling is None else sibling + value
                    else:
                        total = total + value
            s = jnp.concatenate([total, sibling], axis=1)
        s_high, s_low = split(s)
        coefficients = dot_nt(s_high, c_high) + dot_nt(s_low, c_high) + dot_nt(s_high, c_low)
        coefficients = (coefficients * factor).astype(BF16)
        if local == 1 and not last:
            change = jnp.dot(coefficients, g_high, preferred_element_type=F32)
            change = change + jnp.dot(coefficients, g_low, preferred_element_type=F32)
            sums = [products[0:rhs] - change]
            pending = coefficients
            continue
        if local == 1:
            out_copies = []
            for i in range(steps):
                here = pl.ds(i * CHUNK, CHUNK)
                update = jnp.dot(coefficients, basis[n, :, here], preferred_element_type=F32)
                result[:, here] = (source[:, here].astype(F32) - update).astype(BF16)
                out_copies.append(
                    pltpu.make_async_copy(result.at[:, here], out.at[:, here], out_sems.at[i])
                )
                out_copies[-1].start()
            for copy in out_copies:
                copy.wait()
            return
        wait_basis(n + 1)
        next_local = levels[n + 1][2]
        width = steps // local
        sums = []
        for node in range(local):
            mine = coefficients[:, node * RANK : (node + 1) * RANK]

            def step(i, total):
                here = chunk(i)
                update = jnp.dot(mine, basis[n, :, here], preferred_element_type=F32)
                value = source[:, here].astype(F32) - update
                current[:, here] = value
                return total + dot_nt(value.astype(BF16), basis[n + 1, :, here])

            sums.append(
                lax.fori_loop(node * width, (node + 1) * width, step, jnp.zeros((rhs, RANK), F32))
            )
        source = current
        group = local // next_local
        sums = [sum(sums[i * group + 1 : (i + 1) * group], sums[i * group]) for i in range(next_local)]


def shards(right_sides, curve_order, level_bases, capacitance):
    rhs, points = right_sides.shape
    total = points * lax.axis_size(("pts", "sub"))
    levels, slots = plan(points, total)
    hbm = pl.BlockSpec(memory_space=pltpu.MemorySpace.HBM)
    return pl.pallas_call(
        functools.partial(solve_kernel, levels),
        out_shape=jax.ShapeDtypeStruct((rhs, points), BF16),
        in_specs=[hbm, hbm, hbm, hbm],
        out_specs=hbm,
        scratch_shapes=[
            pltpu.VMEM((rhs, points), BF16),
            pltpu.SMEM((1, points), jnp.int32),
            pltpu.VMEM((rhs, points), BF16),
            pltpu.VMEM((points, LANES), F32),
            pltpu.VMEM((LANES, LANES), F32),
            pltpu.VMEM((LANES, LANES), F32),
            pltpu.VMEM((rhs, points), F32),
            pltpu.VMEM((LEVELS, RANK, points), BF16),
            pltpu.VMEM((LEVELS, 2 * RANK, 2 * RANK), F32),
            pltpu.VMEM((rhs, points), BF16),
            pltpu.VMEM((slots, rhs, RANK), BF16),
            pltpu.VMEM((slots, rhs, RANK), BF16),
            pltpu.SemaphoreType.DMA((PIECES + 1,)),
            pltpu.SemaphoreType.DMA((LEVELS,)),
            pltpu.SemaphoreType.DMA((LEVELS,)),
            pltpu.SemaphoreType.DMA((LEVELS,)),
            pltpu.SemaphoreType.DMA((LEVELS, 2)),
            pltpu.SemaphoreType.DMA((points // CHUNK,)),
            pltpu.SemaphoreType.DMA((slots,)),
            pltpu.SemaphoreType.DMA((slots,)),
        ],
        compiler_params=pltpu.CompilerParams(
            collective_id=0, has_side_effects=True, vmem_limit_bytes=58 * 2**20
        ),
        cost_estimate=pl.CostEstimate(
            flops=24 * rhs * RANK * points, bytes_accessed=16 * rhs * points, transcendentals=0
        ),
        name="tree_solve",
    )(right_sides, curve_order, level_bases, capacitance)


def solution(mesh):
    in_specs = (
        P("rep", ("cls", "pts", "sub")),
        P(("cls", "pts", "sub"), None),
        P(None, "rep", ("cls", "pts", "sub")),
        P("cls", None, None),
    )
    out_specs = P("rep", ("cls", "pts", "sub"))
    return jax.shard_map(shards, mesh=mesh, in_specs=in_specs, out_specs=out_specs, check_vma=False)
```

```python
import functools
import math

import jax
import jax.numpy as jnp
from jax import lax
from jax.experimental import pallas as pl
from jax.experimental.pallas import tpu as pltpu
from jax.sharding import PartitionSpec as P

RANK = 128
LEVELS = 4
LANES = 128
CHUNK = 2048
PIECES = 4
STAGE_BITS = 2
MESH = pl.DeviceIdType.MESH
F32 = jnp.float32
BF16 = jnp.bfloat16


def dot_nt(a, b):
    return lax.dot_general(a, b, (((1,), (1,)), ((), ())), preferred_element_type=F32)


def plan(points, total):
    levels, slot = [], 0
    for level in range(LEVELS, 0, -1):
        size = total // 2**level
        span, local = max(size // points, 1), max(points // size, 1)
        stages = []
        if local == 1:
            sibling = span.bit_length() - 1
            bits = list(range(sibling + 1))
            for at in range(0, len(bits), STAGE_BITS):
                group = bits[at : at + STAGE_BITS]
                masks = []
                for mix in range(1, 2 ** len(group)):
                    mask = sum(1 << bit for i, bit in enumerate(group) if mix >> i & 1)
                    masks.append((mask, bool(mask >> sibling & 1), slot))
                    slot += 1
                stages.append(masks)
        factor = 0.3 * 2**level * math.sqrt(size / RANK)
        levels.append((level, span, local, stages, factor))
    return levels, slot


def split(value):
    high = value.astype(BF16)
    return high, (value - high.astype(F32)).astype(BF16)


def gather(order, x, out, table, rows_a, rows_b, first, stop, beside=None, carry=None):
    rhs = x.shape[0]

    table_rows = table.reshape(table.shape[0], 1, LANES)

    def pick(b, rows):
        picked = rows.reshape(LANES, 1, LANES)
        for j in range(LANES):
            picked[j] = table_rows[order[0, b * LANES + j]]

    def put(b, rows):
        cols = pl.ds(pl.multiple_of(b * LANES, LANES), LANES)
        out[:, cols] = rows[...].astype(BF16).T[0:rhs]

    pick(first, rows_a)

    def step(i, carry):
        pick(2 * i + 1, rows_b)
        put(2 * i, rows_a)
        if beside is not None:
            carry = beside(i - first // 2, carry)
        pick(2 * i + 2, rows_a)
        put(2 * i + 1, rows_b)
        return carry

    carry = lax.fori_loop(first // 2, stop // 2 - 1, step, carry)
    pick(stop - 1, rows_b)
    put(stop - 2, rows_a)
    if beside is not None:
        carry = beside((stop - first) // 2 - 1, carry)
    put(stop - 1, rows_b)
    return carry


def solve_kernel(
    levels, sides, order_in, own, cap, out,
    raw, order, x, table, rows_a, rows_b, current, basis, caps, result, send, recv,
    in_sems, basis_sems, far_send_sems, far_recv_sems, cap_sems, out_sems, send_sems, recv_sems,
):
    rhs, points = raw.shape
    half = own.shape[1]
    sub_size = lax.axis_size("sub")
    sub_bits = sub_size.bit_length() - 1
    pts, sub = lax.axis_index("pts"), lax.axis_index("sub")
    rep = lax.axis_index("rep")
    block = pts * sub_size + sub

    def partner(mask):
        def flip(value, bits):
            for i in range(bits.bit_length()):
                if bits >> i & 1:
                    value = value + (1 << i) * (1 - 2 * (value // (1 << i) % 2))
            return value

        return {"pts": flip(pts, mask >> sub_bits), "sub": flip(sub, mask & sub_size - 1)}

    masks = sorted({m for _, _, _, stages, _ in levels for stage in stages for m, _, _ in stage})
    barrier = pltpu.get_barrier_semaphore()
    pl.semaphore_signal(barrier, inc=1, device_id={"rep": 1 - rep}, device_id_type=MESH)
    for mask in masks:
        pl.semaphore_signal(barrier, inc=1, device_id=partner(mask), device_id_type=MESH)

    piece_width = points // PIECES
    side_copies = []
    for piece in range(PIECES):
        cols = pl.ds(piece * piece_width, piece_width)
        side_copies.append(
            pltpu.make_async_copy(sides.at[:, cols], raw.at[:, cols], in_sems.at[piece])
        )
        side_copies[-1].start()
    order_copy = pltpu.make_async_copy(order_in, order, in_sems.at[PIECES])
    order_copy.start()

    basis_copies, cap_copies = [], []
    for n, (level, span, local, _, _) in enumerate(levels):
        first = block // span * local
        parent = 2 ** (level - 1) - 1 + first // 2
        odd = first % 2
        mine_at = basis.at[n, pl.ds(pl.multiple_of(rep * half, half), half), :]
        here = pltpu.make_async_copy(own.at[level - 1], mine_at, basis_sems.at[n])
        far = pltpu.make_async_remote_copy(
            src_ref=own.at[level - 1],
            dst_ref=mine_at,
            send_sem=far_send_sems.at[n],
            recv_sem=far_recv_sems.at[n],
            device_id={"rep": 1 - rep},
            device_id_type=MESH,
        )
        basis_copies.append((here, far))
        if local == 1:
            mine = pl.ds(pl.multiple_of(odd * RANK, RANK), RANK)
            theirs = pl.ds(pl.multiple_of((1 - odd) * RANK, RANK), RANK)
            cap_copies.append(
                [
                    pltpu.make_async_copy(
                        cap.at[parent, mine, cols],
                        caps.at[n, 0:RANK, piece * RANK : (piece + 1) * RANK],
                        cap_sems.at[n, piece],
                    )
                    for piece, cols in enumerate((mine, theirs))
                ]
            )
        else:
            cap_copies.append([pltpu.make_async_copy(cap.at[parent], caps.at[n], cap_sems.at[n, 0])])
        for copy in [here] + cap_copies[-1]:
            copy.start()

    def share_basis():
        pl.semaphore_wait(barrier, len(masks) + 1)
        for _, far in basis_copies:
            far.start()

    @pl.when(rep != 0)
    def _():
        share_basis()

    for piece in range(PIECES):
        side_copies[piece].wait()

        @pl.loop(piece * piece_width // LANES, (piece + 1) * piece_width // LANES, unroll=4)
        def _(b):
            cols = pl.ds(pl.multiple_of(b * LANES, LANES), LANES)
            table[cols, 0:rhs] = raw[:, cols].T.astype(F32)

    order_copy.wait()
    def chunk(i):
        return pl.ds(pl.multiple_of(i * CHUNK, CHUNK), CHUNK)

    steps = points // CHUNK

    def wait_basis(n):
        for copy in basis_copies[n]:
            copy.wait()

    blocks = points // LANES
    local = levels[0][2]
    gather(order, raw, x, table, rows_a, rows_b, 0, blocks // 4)

    @pl.when(rep == 0)
    def _():
        share_basis()

    gather(order, raw, x, table, rows_a, rows_b, blocks // 4, blocks // 2)
    wait_basis(0)

    pair = 2 * LANES
    near = points // 2

    def project(at, total):
        cols = pl.ds(pl.multiple_of(at, pair), pair)
        return total + dot_nt(x[:, cols], basis[0, :, cols])

    def beside(i, totals):
        low, high = totals
        low = project(i * pair, low)
        before = near + i * pair - pair
        cols = pl.ds(pl.multiple_of(before, pair), pair)
        term = dot_nt(x[:, cols], basis[0, :, cols])
        return low, high + jnp.where(i > 0, term, 0.0)

    zero = jnp.zeros((rhs, RANK), F32)
    low, high = gather(
        order, raw, x, table, rows_a, rows_b, blocks // 2, blocks, beside, (zero, zero)
    )
    high = project(points - pair, high)
    sums = [low, high] if local > 1 else [low + high]

    def sweep(n, source, pending):
        ahead = n + 1 < LEVELS
        if ahead:
            wait_basis(n + 1)

        def step(i, total):
            here = chunk(i)
            value = source[:, here]
            if pending is not None:
                value = value - jnp.dot(
                    pending, basis[n - 1, :, here], preferred_element_type=F32
                )
                current[:, here] = value
            if not ahead:
                return total
            left = jnp.concatenate([value.astype(BF16), basis[n, :, here]], axis=0)
            return total + dot_nt(left, basis[n + 1, :, here])

        return lax.fori_loop(0, steps, step, jnp.zeros((rhs + RANK, RANK), F32))

    source, pending = x, None
    for n, (level, span, local, stages, factor) in enumerate(levels):
        last = n == LEVELS - 1
        for copy in cap_copies[n]:
            copy.wait()
        if local > 1:
            s = jnp.concatenate(sums, axis=1)
            c_high, c_low = split(caps[n])
        else:
            total = sums[0]
            sibling = None
            for at, stage in enumerate(stages):
                slot0 = stage[0][2]
                send[slot0] = total.astype(BF16)
                copies = []
                for mask, crosses, slot in stage:
                    copy = pltpu.make_async_remote_copy(
                        src_ref=send.at[slot0],
                        dst_ref=recv.at[slot],
                        send_sem=send_sems.at[slot],
                        recv_sem=recv_sems.at[slot],
                        device_id=partner(mask),
                        device_id_type=MESH,
                    )
                    copy.start()
                    copies.append(copy)
                if at == 0:
                    products = sweep(n, source, pending)
                    if pending is not None:
                        source = current
                    c_high, c_low = split(caps[n, 0:RANK, :])
                    g_high, g_low = split(products[rhs:])
                for copy, (mask, crosses, slot) in zip(copies, stage):
                    copy.wait()
                    value = recv[slot].astype(F32)
                    if crosses:
                        sibling = value if sibling is None else sibling + value
                    else:
                        total = total + value
            s = jnp.concatenate([total, sibling], axis=1)
        s_high, s_low = split(s)
        coefficients = dot_nt(s_high, c_high) + dot_nt(s_low, c_high) + dot_nt(s_high, c_low)
        coefficients = (coefficients * factor).astype(BF16)
        if local == 1 and not last:
            change = jnp.dot(coefficients, g_high, preferred_element_type=F32)
            change = change + jnp.dot(coefficients, g_low, preferred_element_type=F32)
            sums = [products[0:rhs] - change]
            pending = coefficients
            continue
        if local == 1:
            out_copies = []
            for i in range(steps):
                here = pl.ds(i * CHUNK, CHUNK)
                update = jnp.dot(coefficients, basis[n, :, here], preferred_element_type=F32)
                result[:, here] = (source[:, here].astype(F32) - update).astype(BF16)
                out_copies.append(
                    pltpu.make_async_copy(result.at[:, here], out.at[:, here], out_sems.at[i])
                )
                out_copies[-1].start()
            for copy in out_copies:
                copy.wait()
            return
        wait_basis(n + 1)
        next_local = levels[n + 1][2]
        width = steps // local
        sums = []
        for node in range(local):
            mine = coefficients[:, node * RANK : (node + 1) * RANK]

            def step(i, total):
                here = chunk(i)
                update = jnp.dot(mine, basis[n, :, here], preferred_element_type=F32)
                value = source[:, here].astype(F32) - update
                current[:, here] = value
                return total + dot_nt(value.astype(BF16), basis[n + 1, :, here])

            sums.append(
                lax.fori_loop(node * width, (node + 1) * width, step, jnp.zeros((rhs, RANK), F32))
            )
        source = current
        group = local // next_local
        sums = [sum(sums[i * group + 1 : (i + 1) * group], sums[i * group]) for i in range(next_local)]


def shards(right_sides, curve_order, level_bases, capacitance):
    rhs, points = right_sides.shape
    total = points * lax.axis_size(("pts", "sub"))
    levels, slots = plan(points, total)
    hbm = pl.BlockSpec(memory_space=pltpu.MemorySpace.HBM)
    return pl.pallas_call(
        functools.partial(solve_kernel, levels),
        out_shape=jax.ShapeDtypeStruct((rhs, points), BF16),
        in_specs=[hbm, hbm, hbm, hbm],
        out_specs=hbm,
        scratch_shapes=[
            pltpu.VMEM((rhs, points), BF16),
            pltpu.SMEM((1, points), jnp.int32),
            pltpu.VMEM((rhs, points), BF16),
            pltpu.VMEM((points, LANES), F32),
            pltpu.VMEM((LANES, LANES), F32),
            pltpu.VMEM((LANES, LANES), F32),
            pltpu.VMEM((rhs, points), F32),
            pltpu.VMEM((LEVELS, RANK, points), BF16),
            pltpu.VMEM((LEVELS, 2 * RANK, 2 * RANK), F32),
            pltpu.VMEM((rhs, points), BF16),
            pltpu.VMEM((slots, rhs, RANK), BF16),
            pltpu.VMEM((slots, rhs, RANK), BF16),
            pltpu.SemaphoreType.DMA((PIECES + 1,)),
            pltpu.SemaphoreType.DMA((LEVELS,)),
            pltpu.SemaphoreType.DMA((LEVELS,)),
            pltpu.SemaphoreType.DMA((LEVELS,)),
            pltpu.SemaphoreType.DMA((LEVELS, 2)),
            pltpu.SemaphoreType.DMA((points // CHUNK,)),
            pltpu.SemaphoreType.DMA((slots,)),
            pltpu.SemaphoreType.DMA((slots,)),
        ],
        compiler_params=pltpu.CompilerParams(
            collective_id=0, has_side_effects=True, vmem_limit_bytes=58 * 2**20
        ),
        cost_estimate=pl.CostEstimate(
            flops=24 * rhs * RANK * points, bytes_accessed=16 * rhs * points, transcendentals=0
        ),
        name="tree_solve",
    )(right_sides, curve_order, level_bases, capacitance)


def solution(mesh):
    in_specs = (
        P("rep", ("cls", "pts", "sub")),
        P(("cls", "pts", "sub"), None),
        P(None, "rep", ("cls", "pts", "sub")),
        P("cls", None, None),
    )
    out_specs = P("rep", ("cls", "pts", "sub"))
    return jax.shard_map(shards, mesh=mesh, in_specs=in_specs, out_specs=out_specs, check_vma=False)
```
